32 devices in a mesh: groups: 2 (over x), ep: 8 (over z, y), tp: 2 (over core).
Axes of the slice: x: 2, y: 2, z: 4, core: 2. Of those that a mesh axis runs over, the one named last changes fastest.
Arguments:
- queries: bfloat16 [2048, 4096], P(('groups', 'ep'), 'tp'), parts along dimension 0, may hold values from -8 to 8
- keys: bfloat16 [2048, 256], P(('groups', 'ep'), 'tp'), parts along dimension 0, may hold values from -8 to 8
- values: bfloat16 [2048, 256], P(('groups', 'ep'), 'tp'), parts along dimension 0, may hold values from -16 to 16
- norm_gain: float32 [4096], P('tp'), may hold values from 0.5 to 2
- w_gate: bfloat16 [32, 4096, 768], P('ep', None, 'tp'), may hold values from -0.09375 to 0.09375
- w_up: bfloat16 [32, 4096, 768], P('ep', None, 'tp'), may hold values from -0.09375 to 0.09375
- w_down: bfloat16 [32, 768, 4096], P('ep', 'tp'), may hold values from -0.21875 to 0.21875
- expert_ids: int32 [2048, 8], P(('groups', 'ep')), parts along dimension 0, may hold values from 0 to 31, all different within a row; in each aligned block of 128 rows (0 to 127, 128 to 255, ...) at most 40 rows name the same one
- gate_weights: float32 [2048, 8], P(('groups', 'ep')), parts along dimension 0, may hold values from 0.03 to 0.5
Outputs:
- mixed: bfloat16 [2048, 4096], P(('groups', 'ep'), 'tp'), parts along dimension 0
The draws below stay inside these ranges and needn't reach their ends.
There are 2 independent parts, one for each index of `groups`. The reference program is written for one: setup_inputs(seed, part) draws one part's arguments, and reference() takes and returns one part's arrays. A program takes and returns all parts, laid end to end along the dimension named above; an argument that names none is the same for every part. Nothing has to cross between parts.
Inputs may be any that keep to these rules, and one draw needn't show every extreme that they name: `expert_ids`: the 8 experts of a row differ. In the rows of one index of ep no expert is named by more than 40 rows, a bound that some block reaches.
All inputs are finite; a program needn't handle non-finite values.
Results may differ from the reference program's by a relative error of at most 0.01.
Values may be sent and summed in bfloat16 or wider, within the bound.
No kernel may reach another device: no remote copies, remote signals or barrier semaphores. Data moves between devices by JAX's collectives and lax.ppermute only.
A program may use at most 192 MiB of HBM per device.

```python
import math
import jax
import jax.numpy as jnp
import numpy as np
from jax import lax

D = 4096
HEAD_DIMENSION = 128
QUERY_HEAD_COUNT = 32
KEYVALUE_HEADS = 2
FF = 768
EXPERTS = 32
TOP = 8
TOK_DEV = 128
SPAN_TOKENS = 1024
CAP = 40
N_EP = 8


def draw_queries(key, part):
    key = jax.random.fold_in(key, 1)
    rotary_base = jnp.clip(jax.random.normal(key, (SPAN_TOKENS, QUERY_HEAD_COUNT, HEAD_DIMENSION), jnp.float32), -4.0, 4.0)
    return rotary_base.reshape(SPAN_TOKENS, QUERY_HEAD_COUNT * HEAD_DIMENSION).astype(jnp.bfloat16)


def draw_keys(key, part):
    key = jax.random.fold_in(key, 2)
    rotary_base = jnp.clip(jax.random.normal(key, (SPAN_TOKENS, KEYVALUE_HEADS, HEAD_DIMENSION), jnp.float32), -4.0, 4.0)
    return rotary_base.reshape(SPAN_TOKENS, KEYVALUE_HEADS * HEAD_DIMENSION).astype(jnp.bfloat16)


def draw_values(key, part):
    key = jax.random.fold_in(key, 3)
    head_count = jnp.arange(KEYVALUE_HEADS).astype(jnp.float32) / (KEYVALUE_HEADS - 1)
    rotary_base = jnp.clip(jax.random.normal(key, (SPAN_TOKENS, KEYVALUE_HEADS, HEAD_DIMENSION), jnp.float32), -4.0, 4.0)
    scale_factor = 3.0 ** head_count
    return (rotary_base * scale_factor[None, :, None]).reshape(SPAN_TOKENS, KEYVALUE_HEADS * HEAD_DIMENSION).astype(jnp.bfloat16)


def block_scale(own_key, extent, pieces, low, top_value):
    factor_of, own = 1.0, jax.random.fold_in(own_key, 6)
    for axis_at, blocks in pieces:
        heights = jnp.exp(jax.random.uniform(jax.random.fold_in(own, axis_at), (blocks,), jnp.float32, low / len(pieces), top_value / len(pieces)))
        factor_of = factor_of * jnp.repeat(heights, extent[axis_at] // blocks).reshape([-1 if axis == axis_at else 1 for axis in range(len(extent))])
    return factor_of


def shared_out(own_key, own, number, rows, count, top, reach, skew):
    ranking = jax.random.permutation(own_key, count)
    crowded, common = shares(count, rows * top, reach, skew, True), shares(count, rows * top, reach, skew, False)
    places = jnp.arange(count)

    def named(tallies, offset_by):
        used = int((tallies > 0).sum())
        fixed = max(1, used // 4)
        shifted = fixed + (places - fixed + offset_by * (used - fixed)) % max(1, count - fixed)
        return jnp.zeros((count,), jnp.int32).at[ranking[jnp.where(places < fixed, places, shifted)]].set(jnp.asarray(tallies, jnp.int32))

    tallies = jnp.where(number % 4 == 0, named(crowded, number // 4), named(common, number - number // 4 - 1))
    mixed = jax.random.permutation(jax.random.fold_in(own, 3), count)
    donor, sink = mixed[0:count // 2 * 2:2], mixed[1:count // 2 * 2:2]
    slack = jnp.minimum(tallies[donor] - 1, reach - tallies[sink]) // 2
    slack = jnp.where((donor == ranking[0]) | (sink == ranking[0]) | (tallies[sink] == 0), 0, jnp.maximum(slack, 0))
    shifted = jax.random.randint(jax.random.fold_in(own, 4), (count // 2,), 0, 1 << 20) % (slack + 1)
    tallies = tallies.at[donor].add(-shifted).at[sink].add(shifted)
    items = jnp.searchsorted(jnp.cumsum(tallies), jnp.arange(rows * top), side="right").astype(jnp.int32)
    grid = items.reshape(top, rows).T
    grid = grid[jax.random.permutation(jax.random.fold_in(own, 1), rows)]
    offset_by = jax.random.randint(jax.random.fold_in(own, 2), (rows, 1), 0, top)
    return jnp.take_along_axis(grid, (jnp.arange(top)[None, :] + offset_by) % top, axis=1)


def shares(number_of, total, limit, lean, full):
    weights = [(1 << 20) // math.isqrt(grade ** lean) + 1 for grade in range(1, number_of + 1)]
    largest = limit if full else min(limit, max(-(-total // number_of), total * weights[0] // sum(weights)))
    least = 1 if total - largest >= number_of - 1 else 0
    holding, rest = [largest] + [least] * (number_of - 1), total - largest - least * (number_of - 1)
    while rest > 0:
        free = [i for i in range(1, number_of) if holding[i] < largest] or [i for i in range(1, number_of) if holding[i] < limit]
        whole, left = sum([weights[i] for i in free]), rest
        for i in free:
            more = min(limit - holding[i], max(1, left * weights[i] // whole), rest)
            holding[i] = holding[i] + more
            rest = rest - more
    return np.array(holding)


def normal_values(rng, dims, deviation, most, cuts=(), kind=jnp.bfloat16):
    result = deviation * jax.random.normal(rng, dims, jnp.float32)
    if cuts:
        result = result * block_scale(rng, dims, cuts, -0.22, 0.18)
    return jnp.clip(result, -most, most).astype(kind)


def setup_inputs(seed: int = 0, part: int = 0) -> dict:
    arg_keys = jax.random.split(jax.random.key(seed), 10)
    part_splits = jax.random.split(jax.random.fold_in(arg_keys[9], part), 10)
    queries = draw_queries(jax.random.fold_in(jax.random.fold_in(arg_keys[9], part), 71), part)
    keys = draw_keys(jax.random.fold_in(jax.random.fold_in(arg_keys[9], part), 71), part)
    values = draw_values(jax.random.fold_in(jax.random.fold_in(arg_keys[9], part), 71), part)
    norm_gain = jnp.clip(jnp.exp(math.log(2.0) - 1.3862944 * jax.random.uniform(arg_keys[3], (D,), jnp.float32) ** block_scale(arg_keys[3], (D,), ((0, 2),), -0.2, 0.2)), 0.5, 2.0)
    w_gate = normal_values(arg_keys[4], (EXPERTS, D, FF), D ** -0.5, 0.09375, ((0, 8), (2, 2)))
    w_up = normal_values(arg_keys[5], (EXPERTS, D, FF), D ** -0.5, 0.09375, ((0, 8), (2, 2)))
    w_down = normal_values(arg_keys[6], (EXPERTS, FF, D), FF ** -0.5, 0.21875, ((0, 8), (1, 2)))
    expert_ids_keys = jax.random.split(jax.random.fold_in(part_splits[7], 1), SPAN_TOKENS // TOK_DEV)
    expert_ids_turns = jax.random.permutation(jax.random.fold_in(part_splits[7], 3), SPAN_TOKENS // TOK_DEV)
    expert_ids = jax.vmap(lambda own, number: shared_out(jax.random.fold_in(part_splits[7], 2), own, number, TOK_DEV, EXPERTS, TOP, CAP, 2))(expert_ids_keys, expert_ids_turns).reshape((SPAN_TOKENS, TOP))
    gate_weights = jnp.clip(jnp.exp(math.log(0.5) - 2.8134107 * jax.random.uniform(part_splits[8], (SPAN_TOKENS, TOP), jnp.float32) ** block_scale(part_splits[8], (SPAN_TOKENS, TOP), ((0, 8),), -0.2, 0.2)), 0.03, 0.5)
    return {"queries": queries, "keys": keys, "values": values, "norm_gain": norm_gain, "w_gate": w_gate, "w_up": w_up, "w_down": w_down, "expert_ids": expert_ids, "gate_weights": gate_weights}


epsilon = 1e-06

def reference(queries, keys, values, norm_gain, w_gate, w_up, w_down, expert_ids, gate_weights):
    head_group = QUERY_HEAD_COUNT // KEYVALUE_HEADS
    score_scale = 1.0 / math.sqrt(HEAD_DIMENSION)
    positions = jnp.arange(SPAN_TOKENS, dtype=jnp.int32)
    allowed = positions[None, :] <= positions[:, None]

    def one_head(head):
        kv_head = head // head_group
        query_cols = lax.dynamic_slice_in_dim(queries, (head * HEAD_DIMENSION).astype(jnp.int32), HEAD_DIMENSION, 1)
        key_cols = lax.dynamic_slice_in_dim(keys, (kv_head * HEAD_DIMENSION).astype(jnp.int32), HEAD_DIMENSION, 1)
        value_cols = lax.dynamic_slice_in_dim(values, (kv_head * HEAD_DIMENSION).astype(jnp.int32), HEAD_DIMENSION, 1)
        scores = jnp.dot(query_cols, key_cols.T, preferred_element_type=jnp.float32) * score_scale
        scores = jnp.where(allowed, scores, -1e+30)
        top_score = lax.optimization_barrier(jnp.max(scores, axis=1, keepdims=True))
        weights = jnp.where(allowed, jnp.exp(scores - top_score), 0.0)
        totals = lax.optimization_barrier(jnp.sum(weights, axis=1, keepdims=True))
        return jnp.dot(weights.astype(jnp.bfloat16), value_cols, preferred_element_type=jnp.float32) / totals
    heads_out = lax.map(one_head, jnp.arange(QUERY_HEAD_COUNT, dtype=jnp.int32))
    attention = heads_out.transpose(1, 0, 2).reshape(SPAN_TOKENS, D).astype(jnp.bfloat16)
    attn_wide = attention.astype(jnp.float32)
    mean_square = lax.optimization_barrier(jnp.mean(attn_wide * attn_wide, axis=1, keepdims=True))
    normed = (attn_wide * lax.rsqrt(mean_square + epsilon) * norm_gain[None, :]).astype(jnp.bfloat16)
    flat_ids = expert_ids.reshape(-1)
    flat_gates = gate_weights.reshape(-1)
    most_rows = N_EP * CAP

    def one_expert(accum, expert):
        routed = flat_ids == expert
        row_count = jnp.sum(routed.astype(jnp.int32))
        picks = jnp.nonzero(routed, size=most_rows, fill_value=0)[0].astype(jnp.int32)
        filled = jnp.arange(most_rows, dtype=jnp.int32) < row_count
        token_rows = (picks // TOP).astype(jnp.int32)
        inputs = jnp.take(normed, token_rows, axis=0)
        gate_pre = jnp.dot(inputs, w_gate[expert], preferred_element_type=jnp.float32)
        up_pre = jnp.dot(inputs, w_up[expert], preferred_element_type=jnp.float32)
        hidden = (jax.nn.silu(gate_pre) * up_pre).astype(jnp.bfloat16)
        outputs = jnp.dot(hidden, w_down[expert], preferred_element_type=jnp.float32).astype(jnp.bfloat16)
        weight = jnp.where(filled, jnp.take(flat_gates, picks), 0.0)
        accum = accum.at[token_rows].add(weight[:, None] * outputs.astype(jnp.float32))
        return (accum, None)
    accum, unused = lax.scan(one_expert, jnp.zeros((SPAN_TOKENS, D), jnp.float32), jnp.arange(EXPERTS, dtype=jnp.int32))
    return (normed.astype(jnp.float32) + accum).astype(jnp.bfloat16)
```

```python
import functools
import math

import jax
import jax.numpy as jnp
import numpy as np
from jax import lax
from jax.experimental import pallas as pl
from jax.experimental.pallas import tpu as pltpu
from jax.sharding import PartitionSpec as P

HEAD = 128
EXPERTS = 32
TOP = 8
CAP = 40
EPSILON = 1e-06
CHUNKS = 2
F32 = jnp.float32
BF16 = jnp.bfloat16
MIB = 1024 * 1024


def params(mib):
    return pltpu.CompilerParams(vmem_limit_bytes=mib * MIB)


def cost(flops, nbytes, trans=0):
    return pl.CostEstimate(flops=int(flops), bytes_accessed=int(nbytes), transcendentals=int(trans))


class Ring:
    def __init__(self, n_ep):
        self.inner = 2
        self.outer = n_ep // 2
        order = list(range(0, self.outer, 2)) + list(range(1, self.outer, 2))[::-1]
        place = {z: i for i, z in enumerate(order)}
        self.ring_pairs = [
            (order[i] * 2 + y, order[(i + 1) % self.outer] * 2 + y)
            for i in range(self.outer)
            for y in range(2)
        ]
        self.swap_pairs = [(i, i ^ 1) for i in range(n_ep)]
        self.slots = np.array(
            [
                [
                    order[(place[d // 2] - s) % self.outer] * 2 + ((d % 2) ^ y)
                    for s in range(self.outer)
                    for y in range(2)
                ]
                for d in range(n_ep)
            ],
            np.int32,
        )

    def ring(self, x):
        return lax.ppermute(x, "ep", self.ring_pairs)

    def swap(self, x):
        return lax.ppermute(x, "ep", self.swap_pairs)

    def gather(self, x):
        out = []
        for s in range(self.outer):
            if s:
                x = self.ring(x)
            out.append((x, self.swap(x)))
        return out


def core_swap(x):
    return lax.ppermute(x, "tp", [(0, 1), (1, 0)])


def pack_body(k_ref, v_ref, ids_ref, gates_ref, out_ref):
    rows = k_ref.shape[0]
    out_ref[0:rows, :] = k_ref[...]
    out_ref[rows : 2 * rows, :] = v_ref[...]
    ids = ids_ref[...]
    gates = gates_ref[...]
    lane = lax.broadcasted_iota(jnp.int32, (rows, 128), 1)
    named = jnp.zeros((rows, 128), F32)
    weight = jnp.zeros((rows, 128), F32)
    for k in range(TOP):
        hit = ids[:, k : k + 1] == lane
        named = jnp.where(hit, 1.0, named)
        weight = jnp.where(hit, gates[:, k : k + 1], weight)
    named = named.T[:EXPERTS, :]
    weight = weight.T[:EXPERTS, :]
    earlier = lax.broadcasted_iota(jnp.int32, (rows, rows), 0) < lax.broadcasted_iota(
        jnp.int32, (rows, rows), 1
    )
    rank = jnp.dot(
        named.astype(BF16), jnp.where(earlier, 1.0, 0.0).astype(BF16), preferred_element_type=F32
    )
    high = weight.astype(BF16)
    base = 2 * rows
    out_ref[base : base + EXPERTS, :] = jnp.where(named > 0, rank, -1.0).astype(BF16)
    out_ref[base + EXPERTS : base + 2 * EXPERTS, :] = high
    out_ref[base + 2 * EXPERTS : base + 3 * EXPERTS, :] = (weight - high.astype(F32)).astype(BF16)


def pack(keys, values, ids, gates):
    rows = keys.shape[0]
    return pl.pallas_call(
        pack_body,
        out_shape=jax.ShapeDtypeStruct((2 * rows + 3 * EXPERTS, HEAD), BF16),
        compiler_params=params(8),
        cost_estimate=cost(1e6, 300000),
    )(keys, values, ids, gates)


def sort_body(count, local, blocks_ref, *refs):
    slots, (k_ref, v_ref, meta_ref) = refs[:count], refs[count:]
    first = blocks_ref[count]
    row = lax.broadcasted_iota(jnp.int32, (EXPERTS, 128), 0)
    for i in range(count):
        slot = slots[i]
        rows = (slot.shape[0] - 3 * EXPERTS) // 2
        at = pl.multiple_of(blocks_ref[i] * rows, rows)
        k_ref[pl.ds(at, rows), :] = slot[0:rows, :]
        v_ref[pl.ds(at, rows), :] = slot[rows : 2 * rows, :]
        base = 2 * rows
        ranks = slot[base : base + EXPERTS, :].astype(F32)
        weights = slot[base + EXPERTS : base + 2 * EXPERTS, :].astype(F32) + slot[
            base + 2 * EXPERTS : base + 3 * EXPERTS, :
        ].astype(F32)
        for e in range(local):
            mine = row == first + e
            meta_ref[i, e : e + 1, :] = jnp.sum(jnp.where(mine, ranks, 0.0), axis=0, keepdims=True)
            meta_ref[i, 8 + e : 9 + e, :] = jnp.sum(
                jnp.where(mine, weights, 0.0), axis=0, keepdims=True
            )


def sort_slots(blocks, slots, local):
    count = len(slots)
    rows = (slots[0].shape[0] - 3 * EXPERTS) // 2
    vmem = pl.BlockSpec(memory_space=pltpu.VMEM)
    return pl.pallas_call(
        functools.partial(sort_body, count, local),
        out_shape=(
            jax.ShapeDtypeStruct((count * rows, HEAD), BF16),
            jax.ShapeDtypeStruct((count * rows, HEAD), BF16),
            jax.ShapeDtypeStruct((count, 16, 128), F32),
        ),
        in_specs=[pl.BlockSpec(memory_space=pltpu.SMEM)] + [vmem] * count,
        out_specs=(vmem, vmem, vmem),
        compiler_params=params(16),
        cost_estimate=cost(1e6, 2e6),
    )(blocks, *slots)


def attend_body(stack, step, lengths, blocks_ref, q0_ref, q1_ref, k_ref, v_ref, out_ref):
    rows, width = q0_ref.shape
    to_exp2 = math.log2(math.e) / math.sqrt(HEAD)
    for y, q_ref in enumerate((q0_ref, q1_ref)):
        block = blocks_ref[y]
        branch = (block * rows) // step
        for i in range(lengths):
            length = (i + 1) * step

            @pl.when(branch == i)
            def _():
                def some_heads(g, carry):
                    at = pl.multiple_of(g * stack * HEAD, stack * HEAD)
                    wide = q_ref[:, pl.ds(at, stack * HEAD)]
                    q = jnp.concatenate(
                        [wide[:, h * HEAD : (h + 1) * HEAD] for h in range(stack)], axis=0
                    )
                    scores = lax.dot_general(
                        q, k_ref[0:length, :], (((1,), (1,)), ((), ())), preferred_element_type=F32
                    )
                    shape = (stack * rows, step)
                    own = block * rows + (lax.broadcasted_iota(jnp.int32, shape, 0) & (rows - 1))
                    key = (length - step) + lax.broadcasted_iota(jnp.int32, shape, 1)
                    last = jnp.where(key <= own, scores[:, length - step :], -1e30)
                    if i:
                        scores = jnp.concatenate([scores[:, : length - step], last], axis=1)
                    else:
                        scores = last
                    top = jnp.max(scores, axis=1, keepdims=True)
                    probs = jnp.exp2((scores - top) * to_exp2)
                    total = jnp.sum(probs, axis=1, keepdims=True)
                    out = jnp.dot(probs.astype(BF16), v_ref[0:length, :], preferred_element_type=F32)
                    out = (out / total).astype(BF16)
                    for h in range(stack):
                        out_ref[y, :, pl.ds(pl.multiple_of(at + h * HEAD, HEAD), HEAD)] = out[
                            h * rows : (h + 1) * rows, :
                        ]
                    return carry

                lax.fori_loop(0, width // (stack * HEAD), some_heads, 0)


def attend(blocks, q0, q1, k, v):
    rows, width = q0.shape
    total = k.shape[0]
    step = max(256, total // 4)
    vmem = pl.BlockSpec(memory_space=pltpu.VMEM)
    return pl.pallas_call(
        functools.partial(attend_body, 2, step, total // step),
        out_shape=jax.ShapeDtypeStruct((2, rows, width), BF16),
        in_specs=[pl.BlockSpec(memory_space=pltpu.SMEM)] + [vmem] * 4,
        out_specs=vmem,
        compiler_params=params(24),
        cost_estimate=cost(4 * rows * width * total, 4 * rows * width * 2, rows * total * 8),
    )(blocks, q0, q1, k, v)


def one_hot(meta_ref, slot, e, rows):
    first = meta_ref[slot, e : e + 1, :]
    second = meta_ref[slot + 1, e : e + 1, :]
    second = jnp.where(second >= 0, second + CAP, -1.0)
    place = jnp.concatenate([first, second], axis=1)
    row = lax.broadcasted_iota(jnp.int32, (2 * CAP, 2 * rows), 0).astype(F32)
    return row == place


def prep_body(slot, local, width, keep, *refs):
    own, sib = refs[0:CHUNKS], refs[CHUNKS : 2 * CHUNKS]
    gain_refs = refs[2 * CHUNKS : 2 * CHUNKS + 2]
    meta_ref = refs[2 * CHUNKS + 2]
    x_ref = refs[2 * CHUNKS + 3]
    rows, part = own[0].shape[1:]
    scales = []
    for y in range(2):
        squares = jnp.zeros((rows, 1), F32)
        for ref in own + sib:
            a = ref[y].astype(F32)
            squares = squares + jnp.sum(a * a, axis=1, keepdims=True)
        scales.append(lax.rsqrt(squares / width + EPSILON))
    picks = [
        jnp.where(one_hot(meta_ref, slot, e, rows), 1.0, 0.0).astype(BF16) for e in range(local)
    ]
    pick = jnp.concatenate(picks, axis=0)
    for j, half in enumerate((own, sib)):
        for c, ref in enumerate(half):
            gain = gain_refs[j][:, c * part : (c + 1) * part]
            normed = jnp.concatenate(
                [(ref[y].astype(F32) * scales[y] * gain).astype(BF16) for y in range(2)], axis=0
            )
            if keep and j == 0:
                refs[2 * CHUNKS + 4][:, c * part : (c + 1) * part] = normed[:rows]
            x = jnp.dot(pick, normed, preferred_element_type=F32).astype(BF16)
            for e in range(local):
                x_ref[j, e, :, c * part : (c + 1) * part] = x[e * 2 * CAP : (e + 1) * 2 * CAP]


def prepare(slot, own, sib, gain_own, gain_sib, meta, local, keep):
    rows, part = own[0].shape[1:]
    half = part * CHUNKS
    vmem = pl.BlockSpec(memory_space=pltpu.VMEM)
    out_shape = [jax.ShapeDtypeStruct((2, local, 2 * CAP, half), BF16)]
    if keep:
        out_shape.append(jax.ShapeDtypeStruct((rows, half), BF16))
    return pl.pallas_call(
        functools.partial(prep_body, slot, local, 2 * half, keep),
        out_shape=out_shape,
        in_specs=[vmem] * (2 * CHUNKS + 3),
        out_specs=[vmem] * len(out_shape),
        compiler_params=params(24),
        cost_estimate=cost(2 * local * 2 * CAP * 2 * rows * 2 * half, 10e6),
    )(*own, *sib, gain_own, gain_sib, meta)


def up_body(outer, rows, core_ref, *refs):
    xs = refs[:outer]
    gate_ref, up_ref, meta_ref, out_ref, gate_acc, up_acc = refs[outer:]
    e, j = pl.program_id(0), pl.program_id(1)
    x = jnp.concatenate([ref[0, 0] for ref in xs], axis=0)
    gate = jnp.dot(x, gate_ref[0], preferred_element_type=F32)
    up = jnp.dot(x, up_ref[0], preferred_element_type=F32)

    @pl.when(j == 0)
    def _():
        gate_acc[...] = gate
        up_acc[...] = up

    @pl.when(j == 1)
    def _():
        parts = []
        for s in range(outer):
            mask = one_hot_dynamic(meta_ref, 2 * s, e, rows)
            weight = jnp.concatenate(
                [meta_ref[2 * s, pl.ds(8 + e, 1), :], meta_ref[2 * s + 1, pl.ds(8 + e, 1), :]], axis=1
            )
            parts.append(jnp.sum(jnp.where(mask, weight, 0.0), axis=1, keepdims=True))
        weight = jnp.concatenate(parts, axis=0)
        g = gate_acc[...] + gate
        u = up_acc[...] + up
        out_ref[0] = (g / (1.0 + jnp.exp(-g)) * u * weight).astype(BF16)


def one_hot_dynamic(meta_ref, slot, e, rows):
    first = meta_ref[slot, pl.ds(e, 1), :]
    second = meta_ref[slot + 1, pl.ds(e, 1), :]
    second = jnp.where(second >= 0, second + CAP, -1.0)
    place = jnp.concatenate([first, second], axis=1)
    row = lax.broadcasted_iota(jnp.int32, (2 * CAP, 2 * rows), 0).astype(F32)
    return row == place


def up_project(core, xs, w_gate, w_up, meta):
    outer = len(xs)
    _, local, cap2, half = xs[0].shape
    rows = meta.shape[2]
    ff = w_gate.shape[2]
    x_spec = pl.BlockSpec((1, 1, cap2, half), lambda e, j, core: (j, e, 0, 0))
    w_spec = pl.BlockSpec((1, half, ff), lambda e, j, core: (e, core[0] ^ j, 0))
    return pl.pallas_call(
        functools.partial(up_body, outer, rows),
        grid_spec=pltpu.PrefetchScalarGridSpec(
            num_scalar_prefetch=1,
            grid=(local, 2),
            in_specs=[x_spec] * outer
            + [w_spec, w_spec, pl.BlockSpec(meta.shape, lambda e, j, core: (0, 0, 0))],
            out_specs=pl.BlockSpec((1, outer * cap2, ff), lambda e, j, core: (e, 0, 0)),
            scratch_shapes=[
                pltpu.VMEM((outer * cap2, ff), F32),
                pltpu.VMEM((outer * cap2, ff), F32),
            ],
        ),
        out_shape=jax.ShapeDtypeStruct((local, outer * cap2, ff), BF16),
        compiler_params=params(32),
        cost_estimate=cost(
            8 * local * outer * cap2 * half * ff, 4 * local * half * 2 * ff + 4 * outer * cap2 * half
        ),
    )(core, *xs, w_gate, w_up, meta)


def down_body(outer, rows, core_ref, hidden_ref, w_ref, meta_ref, out_ref):
    local = hidden_ref.shape[0]
    ys = [
        jnp.dot(hidden_ref[e], w_ref[e], preferred_element_type=F32).astype(BF16)
        for e in range(local)
    ]
    cap2 = 2 * CAP
    for s in range(outer):
        pick = jnp.concatenate(
            [
                jnp.where(one_hot(meta_ref, 2 * s, e, rows), 1.0, 0.0).astype(BF16)
                for e in range(local)
            ],
            axis=0,
        )
        y = jnp.concatenate([y[s * cap2 : (s + 1) * cap2] for y in ys], axis=0)
        out = lax.dot_general(pick, y, (((0,), (0,)), ((), ())), preferred_element_type=F32)
        out = out.astype(BF16)
        out_ref[2 * s] = out[:rows]
        out_ref[2 * s + 1] = out[rows:]


def down_project(core, hidden, w_down, meta, flip, chunk):
    local, all_rows, ff = hidden.shape
    count, _, rows = meta.shape
    half = w_down.shape[2] // 2
    part = half // CHUNKS
    block = min(512, part)
    steps = part // block
    return pl.pallas_call(
        functools.partial(down_body, count // 2, rows),
        grid_spec=pltpu.PrefetchScalarGridSpec(
            num_scalar_prefetch=1,
            grid=(steps,),
            in_specs=[
                pl.BlockSpec(hidden.shape, lambda n, core: (0, 0, 0)),
                pl.BlockSpec(
                    (local, ff, block),
                    lambda n, core: (
                        0,
                        0,
                        (core[0] ^ flip) * (half // block) + chunk * steps + n,
                    ),
                ),
                pl.BlockSpec(meta.shape, lambda n, core: (0, 0, 0)),
            ],
            out_specs=pl.BlockSpec((count, rows, block), lambda n, core: (0, 0, n)),
        ),
        out_shape=jax.ShapeDtypeStruct((count, rows, part), BF16),
        compiler_params=params(32),
        cost_estimate=cost(
            2 * local * all_rows * ff * part + 4 * count * rows * local * 2 * CAP * part,
            2 * local * ff * part + 2 * count * rows * part,
        ),
    )(core, hidden, w_down, meta)


def shards(ring, queries, keys, values, norm_gain, w_gate, w_up, w_down, expert_ids, gate_weights):
    local = w_gate.shape[0]
    outer = ring.outer
    part = queries.shape[1] // CHUNKS
    me = lax.axis_index("ep")
    core = lax.axis_index("tp").astype(jnp.int32).reshape(1)
    blocks = jnp.asarray(ring.slots)[me]
    sort_scalars = jnp.concatenate([blocks, (me * local).astype(jnp.int32).reshape(1)])

    packed = ring.gather(pack(keys, values, expert_ids, gate_weights))
    query_slots = [ring.gather(queries[:, c * part : (c + 1) * part]) for c in range(CHUNKS)]
    gain_own = norm_gain.reshape(1, -1)
    gain_sib = core_swap(gain_own)
    k, v, meta = sort_slots(sort_scalars, [x for pair in packed for x in pair], local)

    xs = []
    normed = None
    for s in range(outer):
        own = [
            attend(blocks[2 * s : 2 * s + 2], *query_slots[c][s], k, v) for c in range(CHUNKS)
        ]
        sib = [core_swap(x) for x in own]
        made = prepare(2 * s, own, sib, gain_own, gain_sib, meta, local, s == 0)
        xs.append(made[0])
        if s == 0:
            normed = made[1]
    hidden = up_project(core, xs, w_gate, w_up, meta)

    def add(*terms):
        total = terms[0].astype(F32)
        for term in terms[1:]:
            total = total + term.astype(F32)
        return total.astype(BF16)

    outs = []
    for c in range(CHUNKS):
        away = core_swap(down_project(core, hidden, w_down, meta, 1, c))
        here = down_project(core, hidden, w_down, meta, 0, c)
        sums = [None] * outer
        for s in list(range(1, outer)) + [0]:
            other = ring.swap(add(here[2 * s + 1], away[2 * s + 1]))
            sums[s] = (here[2 * s], away[2 * s], other)
        moving = ring.ring(add(*sums[1]))
        for s in range(2, outer):
            moving = ring.ring(add(*sums[s], moving))
        outs.append(add(normed[:, c * part : (c + 1) * part], *sums[0], moving))
    return jnp.concatenate(outs, axis=1)


def solution(mesh):
    ring = Ring(mesh.shape["ep"])
    return jax.shard_map(
        functools.partial(shards, ring),
        mesh=mesh,
        in_specs=(
            P(("groups", "ep"), "tp"),
            P(("groups", "ep"), "tp"),
            P(("groups", "ep"), "tp"),
            P("tp"),
            P("ep", None, "tp"),
            P("ep", None, "tp"),
            P("ep", "tp", None),
            P(("groups", "ep"), None),
            P(("groups", "ep"), None),
        ),
        out_specs=P(("groups", "ep"), "tp"),
        check_vma=False,
    )
```

```python
import functools
import math

import jax
import jax.numpy as jnp
import numpy as np
from jax import lax
from jax.experimental import pallas as pl
from jax.experimental.pallas import tpu as pltpu
from jax.sharding import PartitionSpec as P

HEAD = 128
EXPERTS = 32
TOP = 8
CAP = 40
EPSILON = 1e-06
CHUNKS = 2
F32 = jnp.float32
BF16 = jnp.bfloat16
MIB = 1024 * 1024


def params(mib):
    return pltpu.CompilerParams(vmem_limit_bytes=mib * MIB)


def cost(flops, nbytes, trans=0):
    return pl.CostEstimate(flops=int(flops), bytes_accessed=int(nbytes), transcendentals=int(trans))


class Ring:
    def __init__(self, n_ep):
        self.inner = 2
        self.outer = n_ep // 2
        order = list(range(0, self.outer, 2)) + list(range(1, self.outer, 2))[::-1]
        place = {z: i for i, z in enumerate(order)}
        self.ring_pairs = [
            (order[i] * 2 + y, order[(i + 1) % self.outer] * 2 + y)
            for i in range(self.outer)
            for y in range(2)
        ]
        self.swap_pairs = [(i, i ^ 1) for i in range(n_ep)]
        self.slots = np.array(
            [
                [
                    order[(place[d // 2] - s) % self.outer] * 2 + ((d % 2) ^ y)
                    for s in range(self.outer)
                    for y in range(2)
                ]
                for d in range(n_ep)
            ],
            np.int32,
        )

    def ring(self, x):
        return lax.ppermute(x, "ep", self.ring_pairs)

    def ring_back(self, x):
        return lax.ppermute(x, "ep", [(b, a) for a, b in self.ring_pairs])

    def swap(self, x):
        return lax.ppermute(x, "ep", self.swap_pairs)

    def gather_small(self, x):
        held = {0: x}
        ahead = self.outer // 2
        for s in range(1, ahead + 1):
            held[s] = self.ring(held[s - 1])
        for s in range(1, self.outer - ahead):
            held[self.outer - s] = self.ring_back(held[(self.outer - s + 1) % self.outer])
        return [(held[s], self.swap(held[s])) for s in range(self.outer)]

    def gather(self, x, by_ring):
        out = []
        for s in range(self.outer):
            last = s == self.outer - 1
            if last and by_ring:
                other = self.ring(out[s - 1][1])
            else:
                other = self.swap(x)
            ahead = None if last else self.ring(x)
            out.append((x, other))
            if not last:
                x, kept = lax.optimization_barrier((ahead, other))
                out[s] = (out[s][0], kept)
        return out


def core_swap(x):
    return lax.ppermute(x, "tp", [(0, 1), (1, 0)])


def pack_body(k_ref, v_ref, ids_ref, gates_ref, out_ref):
    rows = k_ref.shape[0]
    out_ref[0:rows, :] = k_ref[...]
    out_ref[rows : 2 * rows, :] = v_ref[...]
    row = lax.broadcasted_iota(jnp.int32, (EXPERTS, rows), 0)
    named = jnp.zeros((EXPERTS, rows), F32)
    weight = jnp.zeros((EXPERTS, rows), F32)
    for k in range(TOP):
        hit = ids_ref[k : k + 1, :] == row
        named = jnp.where(hit, 1.0, named)
        weight = jnp.where(hit, gates_ref[k : k + 1, :], weight)
    earlier = lax.broadcasted_iota(jnp.int32, (rows, rows), 0) < lax.broadcasted_iota(
        jnp.int32, (rows, rows), 1
    )
    rank = jnp.dot(
        named.astype(BF16), jnp.where(earlier, 1.0, 0.0).astype(BF16), preferred_element_type=F32
    )
    high = weight.astype(BF16)
    base = 2 * rows
    out_ref[base : base + EXPERTS, :] = jnp.where(named > 0, rank, -1.0).astype(BF16)
    out_ref[base + EXPERTS : base + 2 * EXPERTS, :] = high
    out_ref[base + 2 * EXPERTS : base + 3 * EXPERTS, :] = (weight - high.astype(F32)).astype(BF16)


def pack(keys, values, ids, gates):
    rows = keys.shape[0]
    return pl.pallas_call(
        pack_body,
        out_shape=jax.ShapeDtypeStruct((2 * rows + 3 * EXPERTS, HEAD), BF16),
        compiler_params=params(8),
        cost_estimate=cost(1e6, 300000),
    )(keys, values, ids, gates)


def sort_body(count, local, blocks_ref, *refs):
    slots, (k_ref, v_ref, meta_ref, turned_ref) = refs[:count], refs[count:]
    first = blocks_ref[count]
    row = lax.broadcasted_iota(jnp.int32, (EXPERTS, 128), 0)
    for i in range(count):
        slot = slots[i]
        rows = (slot.shape[0] - 3 * EXPERTS) // 2
        at = pl.multiple_of(blocks_ref[i] * rows, rows)
        k_ref[pl.ds(at, rows), :] = slot[0:rows, :]
        v_ref[:, pl.ds(at, rows)] = slot[rows : 2 * rows, :].T
        base = 2 * rows
        ranks = slot[base : base + EXPERTS, :].astype(F32)
        weights = slot[base + EXPERTS : base + 2 * EXPERTS, :].astype(F32) + slot[
            base + 2 * EXPERTS : base + 3 * EXPERTS, :
        ].astype(F32)
        picked = []
        for values in (ranks, weights):
            for e in range(8):
                if e < local:
                    mine = jnp.where(row == first + e, values, 0.0)
                    picked.append(jnp.sum(mine, axis=0, keepdims=True))
                else:
                    picked.append(jnp.full((1, 128), -1.0, F32))
        table = jnp.concatenate(picked, axis=0)
        meta_ref[i] = table
        turned_ref[i] = jnp.concatenate([table] * 8, axis=0).T


def sort_slots(blocks, slots, local):
    count = len(slots)
    rows = (slots[0].shape[0] - 3 * EXPERTS) // 2
    vmem = pl.BlockSpec(memory_space=pltpu.VMEM)
    return pl.pallas_call(
        functools.partial(sort_body, count, local),
        out_shape=(
            jax.ShapeDtypeStruct((count * rows, HEAD), BF16),
            jax.ShapeDtypeStruct((HEAD, count * rows), BF16),
            jax.ShapeDtypeStruct((count, 16, 128), F32),
            jax.ShapeDtypeStruct((count, 128, 128), F32),
        ),
        in_specs=[pl.BlockSpec(memory_space=pltpu.SMEM)] + [vmem] * count,
        out_specs=(vmem, vmem, vmem, vmem),
        compiler_params=params(16),
        cost_estimate=cost(1e6, 2e6),
    )(blocks, *slots)


def attend_body(stack, step, lengths, block_ref, q_ref, k_ref, v_ref, out_ref, square_ref):
    rows, width = q_ref.shape
    to_exp2 = math.log2(math.e) / math.sqrt(HEAD)
    block = block_ref[0]
    branch = (block * rows) // step
    square_ref[...] = jnp.zeros(square_ref.shape, F32)
    for i in range(lengths):
        length = (i + 1) * step

        @pl.when(branch == i)
        def _():
            def some_heads(g, carry):
                at = pl.multiple_of(g * (stack * HEAD), stack * HEAD)
                wide = q_ref[:, pl.ds(at, stack * HEAD)]
                q = jnp.concatenate(
                    [wide[:, h * HEAD : (h + 1) * HEAD] for h in range(stack)], axis=0
                )
                scores = lax.dot_general(
                    k_ref[0:length, :], q, (((1,), (1,)), ((), ())), preferred_element_type=F32
                )
                shape = (step, stack * rows)
                own = block * rows + (lax.broadcasted_iota(jnp.int32, shape, 1) & (rows - 1))
                key = (length - step) + lax.broadcasted_iota(jnp.int32, shape, 0)
                last = jnp.where(key <= own, scores[length - step :], -1e30)
                if i:
                    scores = jnp.concatenate([scores[: length - step], last], axis=0)
                else:
                    scores = last
                top = jnp.max(scores, axis=0, keepdims=True)
                probs = jnp.exp2((scores - top) * to_exp2)
                total = jnp.sum(probs, axis=0, keepdims=True)
                out = jnp.dot(v_ref[:, 0:length], probs.astype(BF16), preferred_element_type=F32)
                out = out / total
                squares = jnp.zeros((1, rows), F32)
                turned = []
                for h in range(stack):
                    one = out[:, h * rows : (h + 1) * rows]
                    kept = one.astype(BF16).astype(F32)
                    squares = squares + jnp.sum(kept * kept, axis=0, keepdims=True)
                    turned.append(one.T.astype(BF16))
                out_ref[:, pl.ds(at, stack * HEAD)] = jnp.concatenate(turned, axis=1)
                square_ref[0:1, :] += squares
                return carry

            lax.fori_loop(0, width // (stack * HEAD), some_heads, 0)


def attend(block, q, k, v):
    rows, width = q.shape
    total = k.shape[0]
    step = max(256, total // 4)
    vmem = pl.BlockSpec(memory_space=pltpu.VMEM)
    return pl.pallas_call(
        functools.partial(attend_body, 4, step, total // step),
        out_shape=(
            jax.ShapeDtypeStruct((rows, width), BF16),
            jax.ShapeDtypeStruct((8, rows), F32),
        ),
        in_specs=[pl.BlockSpec(memory_space=pltpu.SMEM)] + [vmem] * 3,
        out_specs=(vmem, vmem),
        compiler_params=params(16),
        cost_estimate=cost(4 * rows * width * total, 4 * rows * width * 2, rows * total * 16),
    )(block, q, k, v)


def norm_body(width, a_ref, own_ref, sib_ref, gain_ref, *out_refs):
    rows, part = out_refs[0].shape
    squares = own_ref[...] + sib_ref[...]
    scale = lax.rsqrt(squares / width + EPSILON)
    scale = jnp.concatenate([scale] * (128 // 8), axis=0).T[:, 0:1]
    for c, ref in enumerate(out_refs):
        cols = slice(c * part, (c + 1) * part)
        ref[...] = (a_ref[:, cols].astype(F32) * scale * gain_ref[:, cols]).astype(BF16)


def normalise(attention, own, sib, gain):
    rows, half = attention.shape
    vmem = pl.BlockSpec(memory_space=pltpu.VMEM)
    return pl.pallas_call(
        functools.partial(norm_body, 2 * half),
        out_shape=[jax.ShapeDtypeStruct((rows, half // CHUNKS), BF16)] * CHUNKS,
        in_specs=[vmem] * 4,
        out_specs=[vmem] * CHUNKS,
        compiler_params=params(8),
        cost_estimate=cost(1e6, 4 * rows * half),
    )(attention, own, sib, gain)


def one_hot(meta_ref, slot, e, rows):
    first = meta_ref[slot, e : e + 1, :]
    second = meta_ref[slot + 1, e : e + 1, :]
    second = jnp.where(second >= 0, second + CAP, -1.0)
    place = jnp.concatenate([first, second], axis=1)
    row = lax.broadcasted_iota(jnp.int32, (2 * CAP, 2 * rows), 0).astype(F32)
    return row == place


def prep_body(slot, local, *refs):
    meta_ref, x_ref = refs[2 * CHUNKS :]
    rows, part = refs[0].shape
    picks = [
        jnp.where(one_hot(meta_ref, slot, e, rows), 1.0, 0.0).astype(BF16) for e in range(local)
    ]
    pick = jnp.concatenate(picks, axis=0)
    for c in range(CHUNKS):
        pair = jnp.concatenate([refs[2 * c][...], refs[2 * c + 1][...]], axis=0)
        x = jnp.dot(pick, pair, preferred_element_type=F32).astype(BF16)
        for e in range(local):
            x_ref[e, :, c * part : (c + 1) * part] = x[e * 2 * CAP : (e + 1) * 2 * CAP]


def prepare(slot, pairs, meta, local):
    rows, part = pairs[0][0].shape
    half = part * CHUNKS
    vmem = pl.BlockSpec(memory_space=pltpu.VMEM)
    return pl.pallas_call(
        functools.partial(prep_body, slot, local),
        out_shape=jax.ShapeDtypeStruct((local, 2 * CAP, half), BF16),
        in_specs=[vmem] * (2 * CHUNKS + 1),
        out_specs=vmem,
        compiler_params=params(12),
        cost_estimate=cost(2 * local * 2 * CAP * 2 * rows * half, 5e6),
    )(*[x for pair in pairs for x in pair], meta)


def one_hot_dynamic(meta_ref, slot, e, rows):
    first = meta_ref[slot, pl.ds(e, 1), :]
    second = meta_ref[slot + 1, pl.ds(e, 1), :]
    second = jnp.where(second >= 0, second + CAP, -1.0)
    place = jnp.concatenate([first, second], axis=1)
    row = lax.broadcasted_iota(jnp.int32, (2 * CAP, 2 * rows), 0).astype(F32)
    return row == place


def experts_body(outer, core_ref, *refs):
    xs = (refs[:outer], refs[outer : 2 * outer])
    gate_ref, up_ref, down_ref, meta_ref, mask_ref = refs[2 * outer : 2 * outer + 5]
    outs = refs[2 * outer + 5 : 2 * outer + 5 + 2 * CHUNKS]
    x_buf, w_buf, d_buf, o_buf, hidden, acc, x_sem, w_sem, d_sem, o_sem = refs[
        2 * outer + 5 + 2 * CHUNKS :
    ]
    local, cap2, half = xs[0][0].shape
    ff = gate_ref.shape[2]
    rows = mask_ref.shape[1]
    wide = o_buf.shape[3]
    block = min(1024, wide)
    per_half = half // block
    per_out = per_half // CHUNKS
    per_flush = wide // block
    core = core_ref[0]

    def x_copy(t, j, s):
        return pltpu.make_async_copy(
            xs[j][s].at[t // 2],
            x_buf.at[j, pl.ds(s * cap2, cap2), :],
            x_sem.at[j, s],
        )

    def w_copy(t, j, i):
        at = pl.multiple_of((core ^ j) * half, half)
        return pltpu.make_async_copy(
            (gate_ref, up_ref)[i].at[t // 2, pl.ds(at, half), :],
            w_buf.at[j, :, pl.ds(i * ff, ff)],
            w_sem.at[j, i],
        )

    def up_copies(t, j):
        return [x_copy(t, j, s) for s in range(outer)] + [w_copy(t, j, i) for i in range(2)]

    def d_copy(e):
        return pltpu.make_async_copy(down_ref.at[e], d_buf.at[e], d_sem.at[e])

    def o_copy(flush, which):
        at = pl.multiple_of((flush % (per_out // per_flush)) * wide, wide)
        return pltpu.make_async_copy(
            o_buf.at[flush % 2], outs[which].at[:, :, pl.ds(at, wide)], o_sem.at[flush % 2]
        )

    for copy in up_copies(0, 0):
        copy.start()

    def up_step(t, carry):
        j = t % 2

        @pl.when(j == 0)
        def _():
            for copy in up_copies(t + 1, 1):
                copy.start()
            for copy in up_copies(t, 0):
                copy.wait()

        @pl.when(j == 1)
        def _():
            @pl.when(t < 2 * local - 1)
            def _():
                for copy in up_copies(t + 1, 0):
                    copy.start()

            d_copy(t // 2).start()

            for copy in up_copies(t, 1):
                copy.wait()

        part = jnp.dot(x_buf[j], w_buf[j], preferred_element_type=F32)

        @pl.when(j == 0)
        def _():
            acc[...] = part

        @pl.when(j == 1)
        def _():
            acc[...] = acc[...] + part
            e = t // 2
            for s in range(outer):
                here = slice(s * cap2, (s + 1) * cap2)
                mask = one_hot_dynamic(meta_ref, 2 * s, e, rows)
                weight = jnp.concatenate(
                    [meta_ref[2 * s + y, pl.ds(8 + e, 1), :] for y in range(2)], axis=1
                )
                weight = jnp.sum(jnp.where(mask, weight, 0.0), axis=1, keepdims=True)
                g = acc[here, 0:ff]
                u = acc[here, ff : 2 * ff]
                hidden[e, here, :] = (g / (1.0 + jnp.exp(-g)) * u * weight).astype(BF16)

        return carry

    lax.fori_loop(0, 2 * local, up_step, 0)

    for e in range(local):
        d_copy(e).wait()

    def down_step(n, carry):
        side = 1 - n // per_half
        at = (core ^ side) * half + (n % per_half) * block
        w_cols = pl.ds(pl.multiple_of(at, block), block)
        o_cols = pl.ds(pl.multiple_of((n % per_flush) * block, block), block)
        flush = n // per_flush
        slot = flush % 2
        ys = [
            jnp.dot(hidden[e], d_buf[e, :, w_cols], preferred_element_type=F32).astype(BF16)
            for e in range(local)
        ]
        for s in range(outer):
            ycat = jnp.concatenate([y[s * cap2 : (s + 1) * cap2] for y in ys], axis=0)
            both = mask_ref[2 * s : 2 * s + 2].reshape(2 * rows, local * cap2)
            out = jnp.dot(both, ycat, preferred_element_type=F32).astype(BF16)
            o_buf[slot, 2 * s, :, o_cols] = out[:rows]
            o_buf[slot, 2 * s + 1, :, o_cols] = out[rows:]
        @pl.when(n % per_flush == per_flush - 1)
        def _():
            for which in range(2 * CHUNKS):

                @pl.when(n // per_out == which)
                def _():
                    o_copy(flush, which).start()

            @pl.when(flush > 0)
            def _():
                o_copy(flush - 1, 0).wait()

        return carry

    lax.fori_loop(0, 2 * per_half, down_step, 0)
    o_copy(2 * per_half // per_flush - 1, 0).wait()


def experts(core, own, sib, w_gate, w_up, w_down, meta, mask):
    outer = len(own)
    local, cap2, half = own[0].shape
    ff = w_gate.shape[2]
    count, rows, _ = mask.shape
    part = half // CHUNKS
    all_rows = outer * cap2
    vmem = pl.BlockSpec(memory_space=pltpu.VMEM)
    anywhere = pl.BlockSpec(memory_space=pl.ANY)
    return pl.pallas_call(
        functools.partial(experts_body, outer),
        in_specs=[pl.BlockSpec(memory_space=pltpu.SMEM)]
        + [anywhere] * (2 * outer + 3)
        + [vmem, vmem],
        out_specs=[anywhere] * (2 * CHUNKS),
        out_shape=[jax.ShapeDtypeStruct((count, rows, part), BF16)] * (2 * CHUNKS),
        scratch_shapes=[
            pltpu.VMEM((2, all_rows, half), BF16),
            pltpu.VMEM((2, half, 2 * ff), BF16),
            pltpu.VMEM((local, ff, 2 * half), BF16),
            pltpu.VMEM((2, count, rows, min(part, 8192 // count)), BF16),
            pltpu.VMEM((local, all_rows, ff), BF16),
            pltpu.VMEM((all_rows, 2 * ff), F32),
            pltpu.SemaphoreType.DMA((2, outer)),
            pltpu.SemaphoreType.DMA((2, 2)),
            pltpu.SemaphoreType.DMA((local,)),
            pltpu.SemaphoreType.DMA((2,)),
        ],
        compiler_params=params(50),
        cost_estimate=cost(
            12 * local * all_rows * half * ff, 12 * local * half * ff + 8 * all_rows * half
        ),
    )(core, *own, *sib, w_gate, w_up, w_down, meta, mask)


def mask_body(local, turned_ref, out_ref):
    _, rows, lanes = out_ref.shape
    lane = lax.broadcasted_iota(jnp.int32, (rows, lanes), 1).astype(F32)
    y = pl.program_id(0) % 2
    hit = jnp.zeros((rows, lanes), F32)
    for e in range(local):
        place = turned_ref[0, :, e : e + 1]
        place = jnp.where(place >= 0, place + (e * 2 * CAP + y * CAP).astype(F32), -1.0)
        hit = jnp.where(lane == place, 1.0, hit)
    out_ref[0] = hit.astype(BF16)


def masks(turned, local):
    count, rows, width = turned.shape
    lanes = local * 2 * CAP
    return pl.pallas_call(
        functools.partial(mask_body, local),
        grid=(count,),
        in_specs=[pl.BlockSpec((1, rows, width), lambda i: (i, 0, 0))],
        out_specs=pl.BlockSpec((1, rows, lanes), lambda i: (i, 0, 0)),
        out_shape=jax.ShapeDtypeStruct((count, rows, lanes), BF16),
        compiler_params=params(8),
        cost_estimate=cost(1e6, count * rows * lanes * 4),
    )(turned)


def shards(ring, queries, keys, values, norm_gain, w_gate, w_up, w_down, expert_ids, gate_weights):
    local = w_gate.shape[0]
    outer = ring.outer
    me = lax.axis_index("ep")
    core = lax.axis_index("tp").astype(jnp.int32).reshape(1)
    blocks = jnp.asarray(ring.slots)[me]
    sort_scalars = jnp.concatenate([blocks, (me * local).astype(jnp.int32).reshape(1)])

    packed = ring.gather_small(pack(keys, values, expert_ids.T, gate_weights.T))
    k, v, meta, turned = sort_slots(sort_scalars, [x for pair in packed for x in pair], local)
    mask = masks(turned, local)
    attention, squares = attend(blocks[:1], queries, k, v)
    normed = normalise(attention, squares, core_swap(squares), norm_gain.reshape(1, -1))
    slots = [ring.gather(normed[c], c == CHUNKS - 1) for c in range(CHUNKS)]
    own = [prepare(2 * s, [slots[c][s] for c in range(CHUNKS)], meta, local) for s in range(outer)]
    sib = [core_swap(x) for x in own]
    parts = experts(core, own, sib, w_gate, w_up, w_down, meta, mask)
    away = [core_swap(x) for x in parts[:CHUNKS]]
    here = parts[CHUNKS:]

    def add(*terms):
        total = terms[0].astype(F32)
        for term in terms[1:]:
            total = total + term.astype(F32)
        return total.astype(BF16)

    firsts = [add(here[c][3], away[c][3]) for c in range(CHUNKS)]
    outs = []
    for c in range(CHUNKS):
        def both(slot):
            return [here[c][slot], away[c][slot]]

        by_ring = c == CHUNKS - 1
        order = list(range(1, outer)) + [0]
        moving, late = [], []
        if by_ring:
            late = [ring.ring(firsts[c])]
            other = []
        else:
            other = [ring.swap(firsts[c])]
        for at, s in enumerate(order):
            if s == 0:
                outs.append(add(normed[c], *both(0), *other, *moving))
                break
            after = order[at + 1]
            send = add(*both(2 * s), *other, *moving)
            extra = late if after == 2 else []
            swapped = add(*both(2 * after + 1), *extra)
            moving, other = [ring.ring(send)], [ring.swap(swapped)]
            pair = lax.optimization_barrier((moving[0], other[0]))
            moving, other = [pair[0]], [pair[1]]
    return jnp.concatenate(outs, axis=1)


def solution(mesh):
    ring = Ring(mesh.shape["ep"])
    return jax.shard_map(
        functools.partial(shards, ring),
        mesh=mesh,
        in_specs=(
            P(("groups", "ep"), "tp"),
            P(("groups", "ep"), "tp"),
            P(("groups", "ep"), "tp"),
            P("tp"),
            P("ep", None, "tp"),
            P("ep", None, "tp"),
            P("ep", "tp", None),
            P(("groups", "ep"), None),
            P(("groups", "ep"), None),
        ),
        out_specs=P(("groups", "ep"), "tp"),
        check_vma=False,
    )
```

```python
import functools
import math

import jax
import jax.numpy as jnp
import numpy as np
from jax import lax
from jax.experimental import pallas as pl
from jax.experimental.pallas import tpu as pltpu
from jax.sharding import PartitionSpec as P

HEAD = 128
EXPERTS = 32
TOP = 8
CAP = 40
EPSILON = 1e-06
CHUNKS = 2
F32 = jnp.float32
BF16 = jnp.bfloat16
MIB = 1024 * 1024


def params(mib):
    return pltpu.CompilerParams(vmem_limit_bytes=mib * MIB)


def cost(flops, nbytes, trans=0):
    return pl.CostEstimate(flops=int(flops), bytes_accessed=int(nbytes), transcendentals=int(trans))


class Ring:
    def __init__(self, n_ep):
        self.inner = 2
        self.outer = n_ep // 2
        order = list(range(0, self.outer, 2)) + list(range(1, self.outer, 2))[::-1]
        place = {z: i for i, z in enumerate(order)}
        self.ring_pairs = [
            (order[i] * 2 + y, order[(i + 1) % self.outer] * 2 + y)
            for i in range(self.outer)
            for y in range(2)
        ]
        self.swap_pairs = [(i, i ^ 1) for i in range(n_ep)]
        self.slots = np.array(
            [
                [
                    order[(place[d // 2] - s) % self.outer] * 2 + ((d % 2) ^ y)
                    for s in range(self.outer)
                    for y in range(2)
                ]
                for d in range(n_ep)
            ],
            np.int32,
        )

    def ring(self, x):
        return lax.ppermute(x, "ep", self.ring_pairs)

    def swap(self, x):
        return lax.ppermute(x, "ep", self.swap_pairs)

    def gather_small(self, x):
        held = [x]
        for s in range(1, self.outer):
            pairs = [(self.slots[d, 2 * s], d) for d in range(len(self.slots))]
            held.append(lax.ppermute(x, "ep", [(int(a), d) for a, d in pairs]))
        return [(x, self.swap(x)) for x in held]

    def gather(self, x, by_ring):
        out = []
        for s in range(self.outer):
            last = s == self.outer - 1
            if last and by_ring:
                other = self.ring(out[s - 1][1])
            else:
                other = self.swap(x)
            ahead = None if last else self.ring(x)
            out.append((x, other))
            if not last:
                x, kept = lax.optimization_barrier((ahead, other))
                out[s] = (out[s][0], kept)
        return out


def core_swap(x):
    return lax.ppermute(x, "tp", [(0, 1), (1, 0)])


def pack_body(k_ref, v_ref, ids_ref, gates_ref, out_ref):
    rows = k_ref.shape[0]
    out_ref[0:rows, :] = k_ref[...]
    out_ref[rows : 2 * rows, :] = v_ref[...]
    row = lax.broadcasted_iota(jnp.int32, (EXPERTS, rows), 0)
    named = jnp.zeros((EXPERTS, rows), F32)
    weight = jnp.zeros((EXPERTS, rows), F32)
    for k in range(TOP):
        hit = ids_ref[k : k + 1, :] == row
        named = jnp.where(hit, 1.0, named)
        weight = jnp.where(hit, gates_ref[k : k + 1, :], weight)
    earlier = lax.broadcasted_iota(jnp.int32, (rows, rows), 0) < lax.broadcasted_iota(
        jnp.int32, (rows, rows), 1
    )
    rank = jnp.dot(
        named.astype(BF16), jnp.where(earlier, 1.0, 0.0).astype(BF16), preferred_element_type=F32
    )
    high = weight.astype(BF16)
    base = 2 * rows
    out_ref[base : base + EXPERTS, :] = jnp.where(named > 0, rank, -1.0).astype(BF16)
    out_ref[base + EXPERTS : base + 2 * EXPERTS, :] = high
    out_ref[base + 2 * EXPERTS : base + 3 * EXPERTS, :] = (weight - high.astype(F32)).astype(BF16)


def pack(keys, values, ids, gates):
    rows = keys.shape[0]
    return pl.pallas_call(
        pack_body,
        out_shape=jax.ShapeDtypeStruct((2 * rows + 3 * EXPERTS, HEAD), BF16),
        compiler_params=params(8),
        cost_estimate=cost(1e6, 300000),
    )(keys, values, ids, gates)


def sort_body(count, local, blocks_ref, *refs):
    slots, (k_ref, v_ref, meta_ref, turned_ref) = refs[:count], refs[count:]
    first = blocks_ref[count]
    row = lax.broadcasted_iota(jnp.int32, (EXPERTS, 128), 0)
    for i in range(count):
        slot = slots[i]
        rows = (slot.shape[0] - 3 * EXPERTS) // 2
        at = pl.multiple_of(blocks_ref[i] * rows, rows)
        k_ref[pl.ds(at, rows), :] = slot[0:rows, :]
        v_ref[:, pl.ds(at, rows)] = slot[rows : 2 * rows, :].T
        base = 2 * rows
        ranks = slot[base : base + EXPERTS, :].astype(F32)
        weights = slot[base + EXPERTS : base + 2 * EXPERTS, :].astype(F32) + slot[
            base + 2 * EXPERTS : base + 3 * EXPERTS, :
        ].astype(F32)
        picked = []
        for values in (ranks, weights):
            for e in range(8):
                if e < local:
                    mine = jnp.where(row == first + e, values, 0.0)
                    picked.append(jnp.sum(mine, axis=0, keepdims=True))
                else:
                    picked.append(jnp.full((1, 128), -1.0, F32))
        table = jnp.concatenate(picked, axis=0)
        meta_ref[i] = table
        turned_ref[i] = jnp.concatenate([table] * 8, axis=0).T


def sort_slots(blocks, slots, local):
    count = len(slots)
    rows = (slots[0].shape[0] - 3 * EXPERTS) // 2
    vmem = pl.BlockSpec(memory_space=pltpu.VMEM)
    return pl.pallas_call(
        functools.partial(sort_body, count, local),
        out_shape=(
            jax.ShapeDtypeStruct((count * rows, HEAD), BF16),
            jax.ShapeDtypeStruct((HEAD, count * rows), BF16),
            jax.ShapeDtypeStruct((count, 16, 128), F32),
            jax.ShapeDtypeStruct((count, 128, 128), F32),
        ),
        in_specs=[pl.BlockSpec(memory_space=pltpu.SMEM)] + [vmem] * count,
        out_specs=(vmem, vmem, vmem, vmem),
        compiler_params=params(16),
        cost_estimate=cost(1e6, 2e6),
    )(blocks, *slots)


def attend_body(stack, step, lengths, block_ref, q_ref, k_ref, v_ref, out_ref, square_ref):
    rows, width = q_ref.shape
    to_exp2 = math.log2(math.e) / math.sqrt(HEAD)
    block = block_ref[0]
    branch = (block * rows) // step
    square_ref[...] = jnp.zeros(square_ref.shape, F32)
    for i in range(lengths):
        length = (i + 1) * step

        @pl.when(branch == i)
        def _():
            def some_heads(g, carry):
                at = pl.multiple_of(g * (stack * HEAD), stack * HEAD)
                wide = q_ref[:, pl.ds(at, stack * HEAD)]
                q = jnp.concatenate(
                    [wide[:, h * HEAD : (h + 1) * HEAD] for h in range(stack)], axis=0
                )
                scores = lax.dot_general(
                    k_ref[0:length, :], q, (((1,), (1,)), ((), ())), preferred_element_type=F32
                )
                shape = (step, stack * rows)
                own = block * rows + (lax.broadcasted_iota(jnp.int32, shape, 1) & (rows - 1))
                key = (length - step) + lax.broadcasted_iota(jnp.int32, shape, 0)
                last = jnp.where(key <= own, scores[length - step :], -1e30)
                if i:
                    scores = jnp.concatenate([scores[: length - step], last], axis=0)
                else:
                    scores = last
                top = jnp.max(scores, axis=0, keepdims=True)
                probs = jnp.exp2((scores - top) * to_exp2)
                total = jnp.sum(probs, axis=0, keepdims=True)
                out = jnp.dot(v_ref[:, 0:length], probs.astype(BF16), preferred_element_type=F32)
                out = out / total
                squares = jnp.zeros((1, rows), F32)
                turned = []
                for h in range(stack):
                    one = out[:, h * rows : (h + 1) * rows]
                    kept = one.astype(BF16).astype(F32)
                    squares = squares + jnp.sum(kept * kept, axis=0, keepdims=True)
                    turned.append(one.T.astype(BF16))
                out_ref[:, pl.ds(at, stack * HEAD)] = jnp.concatenate(turned, axis=1)
                square_ref[0:1, :] += squares
                return carry

            lax.fori_loop(0, width // (stack * HEAD), some_heads, 0)


def attend(block, q, k, v):
    rows, width = q.shape
    total = k.shape[0]
    step = max(256, total // 4)
    vmem = pl.BlockSpec(memory_space=pltpu.VMEM)
    return pl.pallas_call(
        functools.partial(attend_body, 4, step, total // step),
        out_shape=(
            jax.ShapeDtypeStruct((rows, width), BF16),
            jax.ShapeDtypeStruct((8, rows), F32),
        ),
        in_specs=[pl.BlockSpec(memory_space=pltpu.SMEM)] + [vmem] * 3,
        out_specs=(vmem, vmem),
        compiler_params=params(16),
        cost_estimate=cost(4 * rows * width * total, 4 * rows * width * 2, rows * total * 16),
    )(block, q, k, v)


def norm_body(width, a_ref, own_ref, sib_ref, gain_ref, *out_refs):
    rows, part = out_refs[0].shape
    squares = own_ref[...] + sib_ref[...]
    scale = lax.rsqrt(squares / width + EPSILON)
    scale = jnp.concatenate([scale] * (128 // 8), axis=0).T[:, 0:1]
    for c, ref in enumerate(out_refs):
        cols = slice(c * part, (c + 1) * part)
        ref[...] = (a_ref[:, cols].astype(F32) * scale * gain_ref[:, cols]).astype(BF16)


def normalise(attention, own, sib, gain):
    rows, half = attention.shape
    vmem = pl.BlockSpec(memory_space=pltpu.VMEM)
    return pl.pallas_call(
        functools.partial(norm_body, 2 * half),
        out_shape=[jax.ShapeDtypeStruct((rows, half // CHUNKS), BF16)] * CHUNKS,
        in_specs=[vmem] * 4,
        out_specs=[vmem] * CHUNKS,
        compiler_params=params(8),
        cost_estimate=cost(1e6, 4 * rows * half),
    )(attention, own, sib, gain)


def one_hot(meta_ref, slot, e, rows):
    first = meta_ref[slot, e : e + 1, :]
    second = meta_ref[slot + 1, e : e + 1, :]
    second = jnp.where(second >= 0, second + CAP, -1.0)
    place = jnp.concatenate([first, second], axis=1)
    row = lax.broadcasted_iota(jnp.int32, (2 * CAP, 2 * rows), 0).astype(F32)
    return row == place


def prep_body(slot, local, *refs):
    meta_ref, x_ref = refs[2 * CHUNKS :]
    rows, part = refs[0].shape
    picks = [
        jnp.where(one_hot(meta_ref, slot, e, rows), 1.0, 0.0).astype(BF16) for e in range(local)
    ]
    pick = jnp.concatenate(picks, axis=0)
    for c in range(CHUNKS):
        pair = jnp.concatenate([refs[2 * c][...], refs[2 * c + 1][...]], axis=0)
        x = jnp.dot(pick, pair, preferred_element_type=F32).astype(BF16)
        for e in range(local):
            x_ref[e, :, c * part : (c + 1) * part] = x[e * 2 * CAP : (e + 1) * 2 * CAP]


def prepare(slot, pairs, meta, local):
    rows, part = pairs[0][0].shape
    half = part * CHUNKS
    vmem = pl.BlockSpec(memory_space=pltpu.VMEM)
    return pl.pallas_call(
        functools.partial(prep_body, slot, local),
        out_shape=jax.ShapeDtypeStruct((local, 2 * CAP, half), BF16),
        in_specs=[vmem] * (2 * CHUNKS + 1),
        out_specs=vmem,
        compiler_params=params(12),
        cost_estimate=cost(2 * local * 2 * CAP * 2 * rows * half, 5e6),
    )(*[x for pair in pairs for x in pair], meta)


def one_hot_dynamic(meta_ref, slot, e, rows):
    first = meta_ref[slot, pl.ds(e, 1), :]
    second = meta_ref[slot + 1, pl.ds(e, 1), :]
    second = jnp.where(second >= 0, second + CAP, -1.0)
    place = jnp.concatenate([first, second], axis=1)
    row = lax.broadcasted_iota(jnp.int32, (2 * CAP, 2 * rows), 0).astype(F32)
    return row == place


def experts_body(outer, core_ref, *refs):
    xs = (refs[:outer], refs[outer : 2 * outer])
    gate_ref, up_ref, down_ref, meta_ref, mask_ref = refs[2 * outer : 2 * outer + 5]
    y_buf, out_ref, x_buf, w_buf, d_buf, hidden, acc, x_sem, w_sem, d_sem = refs[2 * outer + 5 :]
    local, cap2, half = xs[0][0].shape
    ff = gate_ref.shape[2]
    rows = mask_ref.shape[1]
    core = core_ref[0]

    depth = x_buf.shape[0]
    d_depth = d_buf.shape[0]
    span = 2 * half if outer * cap2 <= 512 else 512

    def x_copy(e, j, s):
        slot = (2 * e + j) % depth
        return pltpu.make_async_copy(
            xs[j][s].at[e], x_buf.at[slot, pl.ds(s * cap2, cap2), :], x_sem.at[slot, s]
        )

    def w_copy(e, j, i):
        slot = (2 * e + j) % depth
        at = pl.multiple_of((core ^ j) * half, half)
        return pltpu.make_async_copy(
            (gate_ref, up_ref)[i].at[e, pl.ds(at, half), :],
            w_buf.at[slot, :, pl.ds(i * ff, ff)],
            w_sem.at[slot, i],
        )

    def up_copies(e, j):
        return [x_copy(e, j, s) for s in range(outer)] + [w_copy(e, j, i) for i in range(2)]

    def d_copy(e):
        return pltpu.make_async_copy(down_ref.at[e], d_buf.at[e % d_depth], d_sem.at[e % d_depth])

    for e in range(depth // 2):
        for copy in up_copies(e, 0) + up_copies(e, 1):
            copy.start()
        if e < d_depth:
            d_copy(e).start()

    def one_expert(e, carry):
        acc[...] = jnp.zeros(acc.shape, F32)

        def one_half(j, inner):
            for side in range(2):

                @pl.when(j == side)
                def _():
                    for copy in up_copies(e, side):
                        copy.wait()

            slot = (2 * e + j) % depth
            acc[...] = acc[...] + jnp.dot(
                x_buf[slot], w_buf[slot], preferred_element_type=F32
            )
            for side in range(2):

                @pl.when((j == side) & (e + depth // 2 < local))
                def _():
                    for copy in up_copies(e + depth // 2, side):
                        copy.start()

            return inner

        lax.fori_loop(0, 2, one_half, 0)
        for s in range(outer):
            here = slice(s * cap2, (s + 1) * cap2)
            mask = one_hot_dynamic(meta_ref, 2 * s, e, rows)
            weight = jnp.concatenate(
                [meta_ref[2 * s + y, pl.ds(8 + e, 1), :] for y in range(2)], axis=1
            )
            weight = jnp.sum(jnp.where(mask, weight, 0.0), axis=1, keepdims=True)
            g = acc[here, 0:ff]
            u = acc[here, ff : 2 * ff]
            hidden[here, :] = (g / (1.0 + jnp.exp(-g)) * u * weight).astype(BF16)
        d_copy(e).wait()

        def columns(n, inner):
            cols = pl.ds(pl.multiple_of(n * span, span), span)
            y = jnp.dot(hidden[...], d_buf[e % d_depth, :, cols], preferred_element_type=F32).astype(BF16)
            for s in range(outer):
                y_buf[s, pl.ds(pl.multiple_of(e * cap2, cap2), cap2), cols] = y[
                    s * cap2 : (s + 1) * cap2
                ]
            return inner

        lax.fori_loop(0, 2 * half // span, columns, 0)

        @pl.when(e + d_depth < local)
        def _():
            d_copy(e + d_depth).start()

        return carry

    lax.fori_loop(0, local, one_expert, 0)

    combine_body([(1, 0)], core_ref, y_buf, mask_ref, out_ref)


def combine_body(parts, core_ref, y_ref, mask_ref, *out_refs):
    outer, all_rows, width = y_ref.shape
    for (flip, chunk), out_ref in zip(parts, out_refs):
        _, rows, part = out_ref.shape
        at = (core_ref[0] ^ flip) * (width // 2) + chunk * part
        cols = pl.ds(pl.multiple_of(at, part), part)
        for s in range(outer):
            both = mask_ref[2 * s : 2 * s + 2].reshape(2 * rows, all_rows)
            out = jnp.dot(both, y_ref[s, :, cols], preferred_element_type=F32).astype(BF16)
            out_ref[2 * s] = out[:rows]
            out_ref[2 * s + 1] = out[rows:]


def combine(core, y, mask, parts):
    count, rows, lanes = mask.shape
    part = y.shape[2] // 2 // CHUNKS
    vmem = pl.BlockSpec(memory_space=pltpu.VMEM)
    return pl.pallas_call(
        functools.partial(combine_body, parts),
        in_specs=[pl.BlockSpec(memory_space=pltpu.SMEM), vmem, vmem],
        out_specs=[vmem] * len(parts),
        out_shape=[jax.ShapeDtypeStruct((count, rows, part), BF16)] * len(parts),
        compiler_params=params(32),
        cost_estimate=cost(
            2 * count * rows * lanes * part * len(parts), 4 * count * rows * part * len(parts)
        ),
    )(core, y, mask)


def experts(core, own, sib, w_gate, w_up, w_down, meta, mask):
    outer = len(own)
    local, cap2, half = own[0].shape
    ff = w_gate.shape[2]
    count, rows, _ = mask.shape
    part = half // CHUNKS
    depth, d_depth = min(4, 2 * local), min(2, local)
    all_rows = outer * cap2
    vmem = pl.BlockSpec(memory_space=pltpu.VMEM)
    anywhere = pl.BlockSpec(memory_space=pl.ANY)
    return pl.pallas_call(
        functools.partial(experts_body, outer),
        in_specs=[pl.BlockSpec(memory_space=pltpu.SMEM)]
        + [anywhere] * (2 * outer + 3)
        + [vmem, vmem],
        out_specs=[vmem, vmem],
        out_shape=[
            pltpu.VMEM((outer, local * cap2, 2 * half), BF16),
            jax.ShapeDtypeStruct((count, rows, part), BF16),
        ],
        scratch_shapes=[
            pltpu.VMEM((depth, all_rows, half), BF16),
            pltpu.VMEM((depth, half, 2 * ff), BF16),
            pltpu.VMEM((d_depth, ff, 2 * half), BF16),
            pltpu.VMEM((all_rows, ff), BF16),
            pltpu.VMEM((all_rows, 2 * ff), F32),
            pltpu.SemaphoreType.DMA((depth, outer)),
            pltpu.SemaphoreType.DMA((depth, 2)),
            pltpu.SemaphoreType.DMA((d_depth,)),
        ],
        compiler_params=params(36 if all_rows <= 512 else 48),
        cost_estimate=cost(
            12 * local * all_rows * half * ff, 12 * local * half * ff + 8 * all_rows * half
        ),
    )(core, *own, *sib, w_gate, w_up, w_down, meta, mask)


def mask_body(local, turned_ref, out_ref):
    _, rows, lanes = out_ref.shape
    lane = lax.broadcasted_iota(jnp.int32, (rows, lanes), 1).astype(F32)
    y = pl.program_id(0) % 2
    hit = jnp.zeros((rows, lanes), F32)
    for e in range(local):
        place = turned_ref[0, :, e : e + 1]
        place = jnp.where(place >= 0, place + (e * 2 * CAP + y * CAP).astype(F32), -1.0)
        hit = jnp.where(lane == place, 1.0, hit)
    out_ref[0] = hit.astype(BF16)


def masks(turned, local):
    count, rows, width = turned.shape
    lanes = local * 2 * CAP
    return pl.pallas_call(
        functools.partial(mask_body, local),
        grid=(count,),
        in_specs=[pl.BlockSpec((1, rows, width), lambda i: (i, 0, 0))],
        out_specs=pl.BlockSpec((1, rows, lanes), lambda i: (i, 0, 0)),
        out_shape=jax.ShapeDtypeStruct((count, rows, lanes), BF16),
        compiler_params=params(8),
        cost_estimate=cost(1e6, count * rows * lanes * 4),
    )(turned)


def shards(ring, queries, keys, values, norm_gain, w_gate, w_up, w_down, expert_ids, gate_weights):
    local = w_gate.shape[0]
    outer = ring.outer
    me = lax.axis_index("ep")
    core = lax.axis_index("tp").astype(jnp.int32).reshape(1)
    blocks = jnp.asarray(ring.slots)[me]
    sort_scalars = jnp.concatenate([blocks, (me * local).astype(jnp.int32).reshape(1)])

    packed = ring.gather_small(pack(keys, values, expert_ids.T, gate_weights.T))
    k, v, meta, turned = sort_slots(sort_scalars, [x for pair in packed for x in pair], local)
    mask = masks(turned, local)
    attention, squares = attend(blocks[:1], queries, k, v)
    normed = normalise(attention, squares, core_swap(squares), norm_gain.reshape(1, -1))
    slots = [ring.gather(normed[c], c == CHUNKS - 1) for c in range(CHUNKS)]
    own = [prepare(2 * s, [slots[c][s] for c in range(CHUNKS)], meta, local) for s in range(outer)]
    sib = [core_swap(x) for x in own]
    y, first = experts(core, own, sib, w_gate, w_up, w_down, meta, mask)
    away, here = [core_swap(first)], []
    for c in range(CHUNKS):
        if c + 1 < CHUNKS:
            mine, other = combine(core, y, mask, [(0, c), (1, c + 1)])
            here.append(mine)
            away.append(core_swap(other))
        else:
            here.append(combine(core, y, mask, [(0, c)])[0])

    def add(*terms):
        total = terms[0].astype(F32)
        for term in terms[1:]:
            total = total + term.astype(F32)
        return total.astype(BF16)

    firsts = [add(here[c][3], away[c][3]) for c in range(CHUNKS)]
    outs = []
    for c in range(CHUNKS):
        def both(slot):
            return [here[c][slot], away[c][slot]]

        by_ring = c == CHUNKS - 1
        order = list(range(1, outer)) + [0]
        moving, late = [], []
        if by_ring:
            late = [ring.ring(firsts[c])]
            other = []
        else:
            other = [ring.swap(firsts[c])]
        for at, s in enumerate(order):
            if s == 0:
                outs.append(add(normed[c], *both(0), *other, *moving))
                break
            after = order[at + 1]
            send = add(*both(2 * s), *other, *moving)
            extra = late if after == 2 else []
            swapped = add(*both(2 * after + 1), *extra)
            moving, other = [ring.ring(send)], [ring.swap(swapped)]
            pair = lax.optimization_barrier((moving[0], other[0]))
            moving, other = [pair[0]], [pair[1]]
    return jnp.concatenate(outs, axis=1)


def solution(mesh):
    ring = Ring(mesh.shape["ep"])
    return jax.shard_map(
        functools.partial(shards, ring),
        mesh=mesh,
        in_specs=(
            P(("groups", "ep"), "tp"),
            P(("groups", "ep"), "tp"),
            P(("groups", "ep"), "tp"),
            P("tp"),
            P("ep", None, "tp"),
            P("ep", None, "tp"),
            P("ep", "tp", None),
            P(("groups", "ep"), None),
            P(("groups", "ep"), None),
        ),
        out_specs=P(("groups", "ep"), "tp"),
        check_vma=False,
    )
```

```python
import functools
import math

import jax
import jax.numpy as jnp
import numpy as np
from jax import lax
from jax.experimental import pallas as pl
from jax.experimental.pallas import tpu as pltpu
from jax.sharding import PartitionSpec as P

HEAD = 128
EXPERTS = 32
TOP = 8
CAP = 40
EPSILON = 1e-06
CHUNKS = 2
F32 = jnp.float32
BF16 = jnp.bfloat16
MIB = 1024 * 1024


def params(mib):
    return pltpu.CompilerParams(vmem_limit_bytes=mib * MIB)


def cost(flops, nbytes, trans=0):
    return pl.CostEstimate(flops=int(flops), bytes_accessed=int(nbytes), transcendentals=int(trans))


class Ring:
    def __init__(self, n_ep):
        self.inner = 2
        self.outer = n_ep // 2
        order = list(range(0, self.outer, 2)) + list(range(1, self.outer, 2))[::-1]
        place = {z: i for i, z in enumerate(order)}
        self.ring_pairs = [
            (order[i] * 2 + y, order[(i + 1) % self.outer] * 2 + y)
            for i in range(self.outer)
            for y in range(2)
        ]
        self.swap_pairs = [(i, i ^ 1) for i in range(n_ep)]
        self.slots = np.array(
            [
                [
                    order[(place[d // 2] - s) % self.outer] * 2 + ((d % 2) ^ y)
                    for s in range(self.outer)
                    for y in range(2)
                ]
                for d in range(n_ep)
            ],
            np.int32,
        )

    def ring(self, x):
        return lax.ppermute(x, "ep", self.ring_pairs)

    def swap(self, x):
        return lax.ppermute(x, "ep", self.swap_pairs)

    def gather_small(self, x):
        held = [x]
        for s in range(1, self.outer):
            pairs = [(self.slots[d, 2 * s], d) for d in range(len(self.slots))]
            held.append(lax.ppermute(x, "ep", [(int(a), d) for a, d in pairs]))
        return [(x, self.swap(x)) for x in held]

    def gather(self, x, by_ring):
        out = []
        for s in range(self.outer):
            last = s == self.outer - 1
            if last and by_ring:
                other = self.ring(out[s - 1][1])
            else:
                other = self.swap(x)
            ahead = None if last else self.ring(x)
            out.append((x, other))
            if not last:
                x, kept = lax.optimization_barrier((ahead, other))
                out[s] = (out[s][0], kept)
        return out


def core_swap(x):
    return lax.ppermute(x, "tp", [(0, 1), (1, 0)])


def pack_body(k_ref, v_ref, ids_ref, gates_ref, out_ref):
    rows = k_ref.shape[0]
    out_ref[0:rows, :] = k_ref[...]
    out_ref[rows : 2 * rows, :] = v_ref[...]
    row = lax.broadcasted_iota(jnp.int32, (EXPERTS, rows), 0)
    named = jnp.zeros((EXPERTS, rows), F32)
    weight = jnp.zeros((EXPERTS, rows), F32)
    for k in range(TOP):
        hit = ids_ref[k : k + 1, :] == row
        named = jnp.where(hit, 1.0, named)
        weight = jnp.where(hit, gates_ref[k : k + 1, :], weight)
    earlier = lax.broadcasted_iota(jnp.int32, (rows, rows), 0) < lax.broadcasted_iota(
        jnp.int32, (rows, rows), 1
    )
    rank = jnp.dot(
        named.astype(BF16), jnp.where(earlier, 1.0, 0.0).astype(BF16), preferred_element_type=F32
    )
    high = weight.astype(BF16)
    base = 2 * rows
    out_ref[base : base + EXPERTS, :] = jnp.where(named > 0, rank, -1.0).astype(BF16)
    out_ref[base + EXPERTS : base + 2 * EXPERTS, :] = high
    out_ref[base + 2 * EXPERTS : base + 3 * EXPERTS, :] = (weight - high.astype(F32)).astype(BF16)


def pack(keys, values, ids, gates):
    rows = keys.shape[0]
    return pl.pallas_call(
        pack_body,
        out_shape=jax.ShapeDtypeStruct((2 * rows + 3 * EXPERTS, HEAD), BF16),
        compiler_params=params(58),
        cost_estimate=cost(1e6, 300000),
    )(keys, values, ids, gates)


def sort_body(count, local, blocks_ref, *refs):
    slots, (k_ref, v_ref, meta_ref, turned_ref) = refs[:count], refs[count:]
    first = blocks_ref[count]
    row = lax.broadcasted_iota(jnp.int32, (EXPERTS, 128), 0)
    for i in range(count):
        slot = slots[i]
        rows = (slot.shape[0] - 3 * EXPERTS) // 2
        at = pl.multiple_of(blocks_ref[i] * rows, rows)
        k_ref[pl.ds(at, rows), :] = slot[0:rows, :]
        v_ref[:, pl.ds(at, rows)] = slot[rows : 2 * rows, :].T
        base = 2 * rows
        ranks = slot[base : base + EXPERTS, :].astype(F32)
        weights = slot[base + EXPERTS : base + 2 * EXPERTS, :].astype(F32) + slot[
            base + 2 * EXPERTS : base + 3 * EXPERTS, :
        ].astype(F32)
        picked = []
        for values in (ranks, weights):
            for e in range(8):
                if e < local:
                    mine = jnp.where(row == first + e, values, 0.0)
                    picked.append(jnp.sum(mine, axis=0, keepdims=True))
                else:
                    picked.append(jnp.full((1, 128), -1.0, F32))
        table = jnp.concatenate(picked, axis=0)
        meta_ref[i] = table
        turned_ref[i] = jnp.concatenate([table] * 8, axis=0).T


def sort_slots(blocks, slots, local):
    count = len(slots)
    rows = (slots[0].shape[0] - 3 * EXPERTS) // 2
    vmem = pl.BlockSpec(memory_space=pltpu.VMEM)
    return pl.pallas_call(
        functools.partial(sort_body, count, local),
        out_shape=(
            jax.ShapeDtypeStruct((count * rows, HEAD), BF16),
            jax.ShapeDtypeStruct((HEAD, count * rows), BF16),
            jax.ShapeDtypeStruct((count, 16, 128), F32),
            jax.ShapeDtypeStruct((count, 128, 128), F32),
        ),
        in_specs=[pl.BlockSpec(memory_space=pltpu.SMEM)] + [vmem] * count,
        out_specs=(vmem, vmem, vmem, vmem),
        compiler_params=params(16),
        cost_estimate=cost(1e6, 2e6),
    )(blocks, *slots)


def attend_body(stack, step, lengths, block_ref, q_ref, k_ref, v_ref, out_ref, square_ref):
    rows, width = q_ref.shape
    to_exp2 = math.log2(math.e) / math.sqrt(HEAD)
    block = block_ref[0]
    branch = (block * rows) // step
    square_ref[...] = jnp.zeros(square_ref.shape, F32)
    for i in range(lengths):
        length = (i + 1) * step

        @pl.when(branch == i)
        def _():
            def some_heads(g, carry):
                at = pl.multiple_of(g * (stack * HEAD), stack * HEAD)
                wide = q_ref[:, pl.ds(at, stack * HEAD)]
                q = jnp.concatenate(
                    [wide[:, h * HEAD : (h + 1) * HEAD] for h in range(stack)], axis=0
                )
                scores = lax.dot_general(
                    k_ref[0:length, :], q, (((1,), (1,)), ((), ())), preferred_element_type=F32
                )
                shape = (step, stack * rows)
                own = block * rows + (lax.broadcasted_iota(jnp.int32, shape, 1) & (rows - 1))
                key = (length - step) + lax.broadcasted_iota(jnp.int32, shape, 0)
                last = jnp.where(key <= own, scores[length - step :], -1e30)
                if i:
                    scores = jnp.concatenate([scores[: length - step], last], axis=0)
                else:
                    scores = last
                top = jnp.max(scores, axis=0, keepdims=True)
                probs = jnp.exp2((scores - top) * to_exp2)
                total = jnp.sum(probs, axis=0, keepdims=True)
                out = jnp.dot(v_ref[:, 0:length], probs.astype(BF16), preferred_element_type=F32)
                out = out / total
                squares = jnp.zeros((1, rows), F32)
                turned = []
                for h in range(stack):
                    one = out[:, h * rows : (h + 1) * rows]
                    kept = one.astype(BF16).astype(F32)
                    squares = squares + jnp.sum(kept * kept, axis=0, keepdims=True)
                    turned.append(one.T.astype(BF16))
                out_ref[:, pl.ds(at, stack * HEAD)] = jnp.concatenate(turned, axis=1)
                square_ref[0:1, :] += squares
                return carry

            lax.fori_loop(0, width // (stack * HEAD), some_heads, 0)


def attend(block, q, k, v):
    rows, width = q.shape
    total = k.shape[0]
    step = max(256, total // 4)
    vmem = pl.BlockSpec(memory_space=pltpu.VMEM)
    return pl.pallas_call(
        functools.partial(attend_body, 8 if total <= 1024 else 4, step, total // step),
        out_shape=(
            jax.ShapeDtypeStruct((rows, width), BF16),
            jax.ShapeDtypeStruct((8, rows), F32),
        ),
        in_specs=[pl.BlockSpec(memory_space=pltpu.SMEM)] + [vmem] * 3,
        out_specs=(vmem, vmem),
        compiler_params=params(16),
        cost_estimate=cost(4 * rows * width * total, 4 * rows * width * 2, rows * total * 16),
    )(block, q, k, v)


def norm_body(width, a_ref, own_ref, sib_ref, gain_ref, *out_refs):
    rows, part = out_refs[0].shape
    squares = own_ref[...] + sib_ref[...]
    scale = lax.rsqrt(squares / width + EPSILON)
    scale = jnp.concatenate([scale] * (128 // 8), axis=0).T[:, 0:1]
    for c, ref in enumerate(out_refs):
        cols = slice(c * part, (c + 1) * part)
        ref[...] = (a_ref[:, cols].astype(F32) * scale * gain_ref[:, cols]).astype(BF16)


def normalise(attention, own, sib, gain):
    rows, half = attention.shape
    vmem = pl.BlockSpec(memory_space=pltpu.VMEM)
    return pl.pallas_call(
        functools.partial(norm_body, 2 * half),
        out_shape=[jax.ShapeDtypeStruct((rows, half // CHUNKS), BF16)] * CHUNKS,
        in_specs=[vmem] * 4,
        out_specs=[vmem] * CHUNKS,
        compiler_params=params(8),
        cost_estimate=cost(1e6, 4 * rows * half),
    )(attention, own, sib, gain)


def one_hot(meta_ref, slot, e, rows):
    first = meta_ref[slot, e : e + 1, :]
    second = meta_ref[slot + 1, e : e + 1, :]
    second = jnp.where(second >= 0, second + CAP, -1.0)
    place = jnp.concatenate([first, second], axis=1)
    row = lax.broadcasted_iota(jnp.int32, (2 * CAP, 2 * rows), 0).astype(F32)
    return row == place


def prep_body(slot, local, *refs):
    meta_ref, x_ref = refs[2 * CHUNKS :]
    rows, part = refs[0].shape
    picks = [
        jnp.where(one_hot(meta_ref, slot, e, rows), 1.0, 0.0).astype(BF16) for e in range(local)
    ]
    pick = jnp.concatenate(picks, axis=0)
    for c in range(CHUNKS):
        pair = jnp.concatenate([refs[2 * c][...], refs[2 * c + 1][...]], axis=0)
        x = jnp.dot(pick, pair, preferred_element_type=F32).astype(BF16)
        for e in range(local):
            x_ref[e, :, c * part : (c + 1) * part] = x[e * 2 * CAP : (e + 1) * 2 * CAP]


def prepare(slot, pairs, meta, local):
    rows, part = pairs[0][0].shape
    half = part * CHUNKS
    vmem = pl.BlockSpec(memory_space=pltpu.VMEM)
    return pl.pallas_call(
        functools.partial(prep_body, slot, local),
        out_shape=jax.ShapeDtypeStruct((local, 2 * CAP, half), BF16),
        in_specs=[vmem] * (2 * CHUNKS + 1),
        out_specs=vmem,
        compiler_params=params(12),
        cost_estimate=cost(2 * local * 2 * CAP * 2 * rows * half, 5e6),
    )(*[x for pair in pairs for x in pair], meta)


def one_hot_dynamic(meta_ref, slot, e, rows):
    first = meta_ref[slot, pl.ds(e, 1), :]
    second = meta_ref[slot + 1, pl.ds(e, 1), :]
    second = jnp.where(second >= 0, second + CAP, -1.0)
    place = jnp.concatenate([first, second], axis=1)
    row = lax.broadcasted_iota(jnp.int32, (2 * CAP, 2 * rows), 0).astype(F32)
    return row == place


def experts_body(outer, core_ref, *refs):
    xs = (refs[:outer], refs[outer : 2 * outer])
    gate_ref, up_ref, down_ref, meta_ref, mask_ref = refs[2 * outer : 2 * outer + 5]
    y_buf, out_ref, x_buf, w_buf, d_buf, hidden, acc, x_sem, w_sem, d_sem = refs[2 * outer + 5 :]
    local, cap2, half = xs[0][0].shape
    ff = gate_ref.shape[2]
    rows = mask_ref.shape[1]
    core = core_ref[0]

    depth = x_buf.shape[0]
    d_depth = d_buf.shape[0]
    span = 2 * half if outer * cap2 <= 512 else 512

    def x_copy(e, j, s):
        slot = (2 * e + j) % depth
        return pltpu.make_async_copy(
            xs[j][s].at[e], x_buf.at[slot, pl.ds(s * cap2, cap2), :], x_sem.at[slot, s]
        )

    def w_copy(e, j, i):
        slot = (2 * e + j) % depth
        at = pl.multiple_of((core ^ j) * half, half)
        return pltpu.make_async_copy(
            (gate_ref, up_ref)[i].at[e, pl.ds(at, half), :],
            w_buf.at[slot, :, pl.ds(i * ff, ff)],
            w_sem.at[slot, i],
        )

    def up_copies(e, j):
        return [x_copy(e, j, s) for s in range(outer)] + [w_copy(e, j, i) for i in range(2)]

    def d_copy(e):
        return pltpu.make_async_copy(down_ref.at[e], d_buf.at[e % d_depth], d_sem.at[e % d_depth])

    for e in range(depth // 2):
        for copy in up_copies(e, 0) + up_copies(e, 1):
            copy.start()
        if e < d_depth:
            d_copy(e).start()

    def one_expert(e, carry):
        acc[...] = jnp.zeros(acc.shape, F32)

        def one_half(j, inner):
            for side in range(2):

                @pl.when(j == side)
                def _():
                    for copy in up_copies(e, side):
                        copy.wait()

            slot = (2 * e + j) % depth
            acc[...] = acc[...] + jnp.dot(
                x_buf[slot], w_buf[slot], preferred_element_type=F32
            )
            for side in range(2):

                @pl.when((j == side) & (e + depth // 2 < local))
                def _():
                    for copy in up_copies(e + depth // 2, side):
                        copy.start()

            return inner

        lax.fori_loop(0, 2, one_half, 0)
        for s in range(outer):
            here = slice(s * cap2, (s + 1) * cap2)
            mask = one_hot_dynamic(meta_ref, 2 * s, e, rows)
            weight = jnp.concatenate(
                [meta_ref[2 * s + y, pl.ds(8 + e, 1), :] for y in range(2)], axis=1
            )
            weight = jnp.sum(jnp.where(mask, weight, 0.0), axis=1, keepdims=True)
            g = acc[here, 0:ff]
            u = acc[here, ff : 2 * ff]
            hidden[here, :] = (g / (1.0 + jnp.exp(-g)) * u * weight).astype(BF16)
        d_copy(e).wait()

        def columns(n, inner):
            cols = pl.ds(pl.multiple_of(n * span, span), span)
            y = jnp.dot(hidden[...], d_buf[e % d_depth, :, cols], preferred_element_type=F32).astype(BF16)
            for s in range(outer):
                y_buf[s, pl.ds(pl.multiple_of(e * cap2, cap2), cap2), cols] = y[
                    s * cap2 : (s + 1) * cap2
                ]
            return inner

        lax.fori_loop(0, 2 * half // span, columns, 0)

        @pl.when(e + d_depth < local)
        def _():
            d_copy(e + d_depth).start()

        return carry

    lax.fori_loop(0, local, one_expert, 0)

    combine_body([(1, 0)], core_ref, y_buf, mask_ref, out_ref)


def combine_body(parts, core_ref, y_ref, mask_ref, *out_refs):
    outer, all_rows, width = y_ref.shape
    for (flip, chunk), out_ref in zip(parts, out_refs):
        _, rows, part = out_ref.shape
        at = (core_ref[0] ^ flip) * (width // 2) + chunk * part
        cols = pl.ds(pl.multiple_of(at, part), part)
        for s in range(outer):
            both = mask_ref[2 * s : 2 * s + 2].reshape(2 * rows, all_rows)
            out = jnp.dot(both, y_ref[s, :, cols], preferred_element_type=F32).astype(BF16)
            out_ref[2 * s] = out[:rows]
            out_ref[2 * s + 1] = out[rows:]


def combine(core, y, mask, parts):
    count, rows, lanes = mask.shape
    part = y.shape[2] // 2 // CHUNKS
    vmem = pl.BlockSpec(memory_space=pltpu.VMEM)
    return pl.pallas_call(
        functools.partial(combine_body, parts),
        in_specs=[pl.BlockSpec(memory_space=pltpu.SMEM), vmem, vmem],
        out_specs=[vmem] * len(parts),
        out_shape=[jax.ShapeDtypeStruct((count, rows, part), BF16)] * len(parts),
        compiler_params=params(32),
        cost_estimate=cost(
            2 * count * rows * lanes * part * len(parts), 4 * count * rows * part * len(parts)
        ),
    )(core, y, mask)


def experts(core, own, sib, w_gate, w_up, w_down, meta, mask):
    outer = len(own)
    local, cap2, half = own[0].shape
    ff = w_gate.shape[2]
    count, rows, _ = mask.shape
    part = half // CHUNKS
    depth, d_depth = min(4, 2 * local), min(2, local)
    all_rows = outer * cap2
    vmem = pl.BlockSpec(memory_space=pltpu.VMEM)
    anywhere = pl.BlockSpec(memory_space=pl.ANY)
    return pl.pallas_call(
        functools.partial(experts_body, outer),
        in_specs=[pl.BlockSpec(memory_space=pltpu.SMEM)]
        + [anywhere] * (2 * outer + 3)
        + [vmem, vmem],
        out_specs=[vmem, vmem],
        out_shape=[
            pltpu.VMEM((outer, local * cap2, 2 * half), BF16),
            jax.ShapeDtypeStruct((count, rows, part), BF16),
        ],
        scratch_shapes=[
            pltpu.VMEM((depth, all_rows, half), BF16),
            pltpu.VMEM((depth, half, 2 * ff), BF16),
            pltpu.VMEM((d_depth, ff, 2 * half), BF16),
            pltpu.VMEM((all_rows, ff), BF16),
            pltpu.VMEM((all_rows, 2 * ff), F32),
            pltpu.SemaphoreType.DMA((depth, outer)),
            pltpu.SemaphoreType.DMA((depth, 2)),
            pltpu.SemaphoreType.DMA((d_depth,)),
        ],
        compiler_params=params(36 if all_rows <= 512 else 48),
        cost_estimate=cost(
            12 * local * all_rows * half * ff, 12 * local * half * ff + 8 * all_rows * half
        ),
    )(core, *own, *sib, w_gate, w_up, w_down, meta, mask)


def mask_body(local, turned_ref, out_ref):
    _, rows, lanes = out_ref.shape
    lane = lax.broadcasted_iota(jnp.int32, (rows, lanes), 1).astype(F32)
    y = pl.program_id(0) % 2
    hit = jnp.zeros((rows, lanes), F32)
    for e in range(local):
        place = turned_ref[0, :, e : e + 1]
        place = jnp.where(place >= 0, place + (e * 2 * CAP + y * CAP).astype(F32), -1.0)
        hit = jnp.where(lane == place, 1.0, hit)
    out_ref[0] = hit.astype(BF16)


def masks(turned, local):
    count, rows, width = turned.shape
    lanes = local * 2 * CAP
    return pl.pallas_call(
        functools.partial(mask_body, local),
        grid=(count,),
        in_specs=[pl.BlockSpec((1, rows, width), lambda i: (i, 0, 0))],
        out_specs=pl.BlockSpec((1, rows, lanes), lambda i: (i, 0, 0)),
        out_shape=jax.ShapeDtypeStruct((count, rows, lanes), BF16),
        compiler_params=params(8),
        cost_estimate=cost(1e6, count * rows * lanes * 4),
    )(turned)


def shards(ring, queries, keys, values, norm_gain, w_gate, w_up, w_down, expert_ids, gate_weights):
    local = w_gate.shape[0]
    outer = ring.outer
    me = lax.axis_index("ep")
    core = lax.axis_index("tp").astype(jnp.int32).reshape(1)
    blocks = jnp.asarray(ring.slots)[me]
    sort_scalars = jnp.concatenate([blocks, (me * local).astype(jnp.int32).reshape(1)])

    packed = ring.gather_small(pack(keys, values, expert_ids.T, gate_weights.T))
    k, v, meta, turned = sort_slots(sort_scalars, [x for pair in packed for x in pair], local)
    mask = masks(turned, local)
    attention, squares = attend(blocks[:1], queries, k, v)
    normed = normalise(attention, squares, core_swap(squares), norm_gain.reshape(1, -1))
    slots = [ring.gather(normed[c], c == CHUNKS - 1) for c in range(CHUNKS)]
    own = [prepare(2 * s, [slots[c][s] for c in range(CHUNKS)], meta, local) for s in range(outer)]
    sib = [core_swap(x) for x in own]
    y, first = experts(core, own, sib, w_gate, w_up, w_down, meta, mask)
    away, here = [core_swap(first)], []
    for c in range(CHUNKS):
        if c + 1 < CHUNKS:
            mine, other = combine(core, y, mask, [(0, c), (1, c + 1)])
            here.append(mine)
            away.append(core_swap(other))
        else:
            here.append(combine(core, y, mask, [(0, c)])[0])

    def add(*terms):
        total = terms[0].astype(F32)
        for term in terms[1:]:
            total = total + term.astype(F32)
        return total.astype(BF16)

    firsts = [add(here[c][3], away[c][3]) for c in range(CHUNKS)]
    outs = []
    for c in range(CHUNKS):
        def both(slot):
            return [here[c][slot], away[c][slot]]

        by_ring = c == CHUNKS - 1
        order = list(range(1, outer)) + [0]
        moving, late = [], []
        if by_ring:
            late = [ring.ring(firsts[c])]
            other = []
        else:
            other = [ring.swap(firsts[c])]
        for at, s in enumerate(order):
            if s == 0:
                outs.append(add(normed[c], *both(0), *other, *moving))
                break
            after = order[at + 1]
            send = add(*both(2 * s), *other, *moving)
            extra = late if after == 2 else []
            swapped = add(*both(2 * after + 1), *extra)
            moving, other = [ring.ring(send)], [ring.swap(swapped)]
            pair = lax.optimization_barrier((moving[0], other[0]))
            moving, other = [pair[0]], [pair[1]]
    return jnp.concatenate(outs, axis=1)


def solution(mesh):
    ring = Ring(mesh.shape["ep"])
    return jax.shard_map(
        functools.partial(shards, ring),
        mesh=mesh,
        in_specs=(
            P(("groups", "ep"), "tp"),
            P(("groups", "ep"), "tp"),
            P(("groups", "ep"), "tp"),
            P("tp"),
            P("ep", None, "tp"),
            P("ep", None, "tp"),
            P("ep", "tp", None),
            P(("groups", "ep"), None),
            P(("groups", "ep"), None),
        ),
        out_specs=P(("groups", "ep"), "tp"),
        check_vma=False,
    )
```

```python
import functools
import math

import jax
import jax.numpy as jnp
import numpy as np
from jax import lax
from jax.experimental import pallas as pl
from jax.experimental.pallas import tpu as pltpu
from jax.sharding import PartitionSpec as P

HEAD = 128
EXPERTS = 32
TOP = 8
CAP = 40
EPSILON = 1e-06
CHUNKS = 2
F32 = jnp.float32
BF16 = jnp.bfloat16
MIB = 1024 * 1024


def params(mib):
    return pltpu.CompilerParams(vmem_limit_bytes=mib * MIB)


def cost(flops, nbytes, trans=0):
    return pl.CostEstimate(flops=int(flops), bytes_accessed=int(nbytes), transcendentals=int(trans))


class Ring:
    def __init__(self, n_ep):
        self.inner = 2
        self.outer = n_ep // 2
        order = list(range(0, self.outer, 2)) + list(range(1, self.outer, 2))[::-1]
        place = {z: i for i, z in enumerate(order)}
        self.ring_pairs = [
            (order[i] * 2 + y, order[(i + 1) % self.outer] * 2 + y)
            for i in range(self.outer)
            for y in range(2)
        ]
        self.swap_pairs = [(i, i ^ 1) for i in range(n_ep)]
        self.slots = np.array(
            [
                [
                    order[(place[d // 2] - s) % self.outer] * 2 + ((d % 2) ^ y)
                    for s in range(self.outer)
                    for y in range(2)
                ]
                for d in range(n_ep)
            ],
            np.int32,
        )

    def ring(self, x):
        return lax.ppermute(x, "ep", self.ring_pairs)

    def swap(self, x):
        return lax.ppermute(x, "ep", self.swap_pairs)

    def gather_small(self, x):
        held = [x]
        for s in range(1, self.outer):
            pairs = [(self.slots[d, 2 * s], d) for d in range(len(self.slots))]
            held.append(lax.ppermute(x, "ep", [(int(a), d) for a, d in pairs]))
        return [(x, self.swap(x)) for x in held]

    def gather(self, x, by_ring):
        out = []
        for s in range(self.outer):
            last = s == self.outer - 1
            if last and by_ring:
                other = self.ring(out[s - 1][1])
            else:
                other = self.swap(x)
            ahead = None if last else self.ring(x)
            out.append((x, other))
            if not last:
                x, kept = lax.optimization_barrier((ahead, other))
                out[s] = (out[s][0], kept)
        return out


def core_swap(x):
    return lax.ppermute(x, "tp", [(0, 1), (1, 0)])


def pack_body(k_ref, v_ref, ids_ref, gates_ref, out_ref):
    rows = k_ref.shape[0]
    out_ref[0:rows, :] = k_ref[...]
    out_ref[rows : 2 * rows, :] = v_ref[...]
    row = lax.broadcasted_iota(jnp.int32, (EXPERTS, rows), 0)
    named = jnp.zeros((EXPERTS, rows), F32)
    weight = jnp.zeros((EXPERTS, rows), F32)
    for k in range(TOP):
        hit = ids_ref[k : k + 1, :] == row
        named = jnp.where(hit, 1.0, named)
        weight = jnp.where(hit, gates_ref[k : k + 1, :], weight)
    earlier = lax.broadcasted_iota(jnp.int32, (rows, rows), 0) < lax.broadcasted_iota(
        jnp.int32, (rows, rows), 1
    )
    rank = jnp.dot(
        named.astype(BF16), jnp.where(earlier, 1.0, 0.0).astype(BF16), preferred_element_type=F32
    )
    high = weight.astype(BF16)
    base = 2 * rows
    out_ref[base : base + EXPERTS, :] = jnp.where(named > 0, rank, -1.0).astype(BF16)
    out_ref[base + EXPERTS : base + 2 * EXPERTS, :] = high
    out_ref[base + 2 * EXPERTS : base + 3 * EXPERTS, :] = (weight - high.astype(F32)).astype(BF16)


def pack(keys, values, ids, gates):
    rows = keys.shape[0]
    return pl.pallas_call(
        pack_body,
        out_shape=jax.ShapeDtypeStruct((2 * rows + 3 * EXPERTS, HEAD), BF16),
        compiler_params=params(58),
        cost_estimate=cost(1e6, 300000),
    )(keys, values, ids, gates)


def sort_body(count, local, blocks_ref, *refs):
    slots, (k_ref, v_ref, meta_ref) = refs[:count], refs[count:]
    first = blocks_ref[count]
    row = lax.broadcasted_iota(jnp.int32, (EXPERTS, 128), 0)
    for i in range(count):
        slot = slots[i]
        rows = (slot.shape[0] - 3 * EXPERTS) // 2
        at = pl.multiple_of(blocks_ref[i] * rows, rows)
        k_ref[pl.ds(at, rows), :] = slot[0:rows, :]
        v_ref[:, pl.ds(at, rows)] = slot[rows : 2 * rows, :].T
        base = 2 * rows
        ranks = slot[base : base + EXPERTS, :].astype(F32)
        weights = slot[base + EXPERTS : base + 2 * EXPERTS, :].astype(F32) + slot[
            base + 2 * EXPERTS : base + 3 * EXPERTS, :
        ].astype(F32)
        picked = []
        for values in (ranks, weights):
            for e in range(8):
                if e < local:
                    mine = jnp.where(row == first + e, values, 0.0)
                    picked.append(jnp.sum(mine, axis=0, keepdims=True))
                else:
                    picked.append(jnp.full((1, 128), -1.0, F32))
        table = jnp.concatenate(picked, axis=0)
        meta_ref[i] = table


def sort_slots(blocks, slots, local):
    count = len(slots)
    rows = (slots[0].shape[0] - 3 * EXPERTS) // 2
    vmem = pl.BlockSpec(memory_space=pltpu.VMEM)
    return pl.pallas_call(
        functools.partial(sort_body, count, local),
        out_shape=(
            jax.ShapeDtypeStruct((count * rows, HEAD), BF16),
            jax.ShapeDtypeStruct((HEAD, count * rows), BF16),
            jax.ShapeDtypeStruct((count, 16, 128), F32),
        ),
        in_specs=[pl.BlockSpec(memory_space=pltpu.SMEM)] + [vmem] * count,
        out_specs=(vmem, vmem, vmem),
        compiler_params=params(16),
        cost_estimate=cost(1e6, 2e6),
    )(blocks, *slots)


def attend_body(stack, step, lengths, block_ref, q_ref, k_ref, v_ref, out_ref, square_ref):
    rows, width = q_ref.shape
    to_exp2 = math.log2(math.e) / math.sqrt(HEAD)
    block = block_ref[0]
    branch = (block * rows) // step
    square_ref[...] = jnp.zeros(square_ref.shape, F32)
    for i in range(lengths):
        length = (i + 1) * step

        @pl.when(branch == i)
        def _():
            def some_heads(g, carry):
                at = pl.multiple_of(g * (stack * HEAD), stack * HEAD)
                wide = q_ref[:, pl.ds(at, stack * HEAD)]
                q = jnp.concatenate(
                    [wide[:, h * HEAD : (h + 1) * HEAD] for h in range(stack)], axis=0
                )
                scores = lax.dot_general(
                    k_ref[0:length, :], q, (((1,), (1,)), ((), ())), preferred_element_type=F32
                )
                shape = (step, stack * rows)
                own = block * rows + (lax.broadcasted_iota(jnp.int32, shape, 1) & (rows - 1))
                key = (length - step) + lax.broadcasted_iota(jnp.int32, shape, 0)
                last = jnp.where(key <= own, scores[length - step :], -1e30)
                if i:
                    scores = jnp.concatenate([scores[: length - step], last], axis=0)
                else:
                    scores = last
                top = jnp.max(scores, axis=0, keepdims=True)
                probs = jnp.exp2((scores - top) * to_exp2)
                total = jnp.sum(probs, axis=0, keepdims=True)
                out = jnp.dot(v_ref[:, 0:length], probs.astype(BF16), preferred_element_type=F32)
                out = out / total
                squares = jnp.zeros((1, rows), F32)
                turned = []
                for h in range(stack):
                    one = out[:, h * rows : (h + 1) * rows]
                    kept = one.astype(BF16).astype(F32)
                    squares = squares + jnp.sum(kept * kept, axis=0, keepdims=True)
                    turned.append(one.T.astype(BF16))
                out_ref[:, pl.ds(at, stack * HEAD)] = jnp.concatenate(turned, axis=1)
                square_ref[0:1, :] += squares
                return carry

            lax.fori_loop(0, width // (stack * HEAD), some_heads, 0)


def attend(block, q, k, v):
    rows, width = q.shape
    total = k.shape[0]
    step = max(256, total // 4)
    vmem = pl.BlockSpec(memory_space=pltpu.VMEM)
    return pl.pallas_call(
        functools.partial(attend_body, 8 if total <= 1024 else 4, step, total // step),
        out_shape=(
            jax.ShapeDtypeStruct((rows, width), BF16),
            jax.ShapeDtypeStruct((8, rows), F32),
        ),
        in_specs=[pl.BlockSpec(memory_space=pltpu.SMEM)] + [vmem] * 3,
        out_specs=(vmem, vmem),
        compiler_params=params(16),
        cost_estimate=cost(4 * rows * width * total, 4 * rows * width * 2, rows * total * 16),
    )(block, q, k, v)


def norm_body(width, a_ref, own_ref, sib_ref, gain_ref, *out_refs):
    rows, part = out_refs[0].shape
    squares = own_ref[...] + sib_ref[...]
    scale = lax.rsqrt(squares / width + EPSILON)
    scale = jnp.concatenate([scale] * (128 // 8), axis=0).T[:, 0:1]
    for c, ref in enumerate(out_refs):
        cols = slice(c * part, (c + 1) * part)
        ref[...] = (a_ref[:, cols].astype(F32) * scale * gain_ref[:, cols]).astype(BF16)


def normalise(attention, own, sib, gain):
    rows, half = attention.shape
    vmem = pl.BlockSpec(memory_space=pltpu.VMEM)
    return pl.pallas_call(
        functools.partial(norm_body, 2 * half),
        out_shape=[jax.ShapeDtypeStruct((rows, half // CHUNKS), BF16)] * CHUNKS,
        in_specs=[vmem] * 4,
        out_specs=[vmem] * CHUNKS,
        compiler_params=params(8),
        cost_estimate=cost(1e6, 4 * rows * half),
    )(attention, own, sib, gain)


def one_hot(meta_ref, slot, e, rows):
    first = meta_ref[slot, e : e + 1, :]
    second = meta_ref[slot + 1, e : e + 1, :]
    second = jnp.where(second >= 0, second + CAP, -1.0)
    place = jnp.concatenate([first, second], axis=1)
    row = lax.broadcasted_iota(jnp.int32, (2 * CAP, 2 * rows), 0).astype(F32)
    return row == place


def prep_body(slot, local, *refs):
    meta_ref, x_ref = refs[2 * CHUNKS :]
    rows, part = refs[0].shape
    picks = [
        jnp.where(one_hot(meta_ref, slot, e, rows), 1.0, 0.0).astype(BF16) for e in range(local)
    ]
    pick = jnp.concatenate(picks, axis=0)
    for c in range(CHUNKS):
        pair = jnp.concatenate([refs[2 * c][...], refs[2 * c + 1][...]], axis=0)
        x = jnp.dot(pick, pair, preferred_element_type=F32).astype(BF16)
        for e in range(local):
            x_ref[e, :, c * part : (c + 1) * part] = x[e * 2 * CAP : (e + 1) * 2 * CAP]


def prepare(slot, pairs, meta, local):
    rows, part = pairs[0][0].shape
    half = part * CHUNKS
    vmem = pl.BlockSpec(memory_space=pltpu.VMEM)
    return pl.pallas_call(
        functools.partial(prep_body, slot, local),
        out_shape=jax.ShapeDtypeStruct((local, 2 * CAP, half), BF16),
        in_specs=[vmem] * (2 * CHUNKS + 1),
        out_specs=vmem,
        compiler_params=params(12),
        cost_estimate=cost(2 * local * 2 * CAP * 2 * rows * half, 5e6),
    )(*[x for pair in pairs for x in pair], meta)


def one_hot_dynamic(meta_ref, slot, e, rows):
    first = meta_ref[slot, pl.ds(e, 1), :]
    second = meta_ref[slot + 1, pl.ds(e, 1), :]
    second = jnp.where(second >= 0, second + CAP, -1.0)
    place = jnp.concatenate([first, second], axis=1)
    row = lax.broadcasted_iota(jnp.int32, (2 * CAP, 2 * rows), 0).astype(F32)
    return row == place


def experts_body(outer, core_ref, *refs):
    xs = (refs[:outer], refs[outer : 2 * outer])
    gate_ref, up_ref, down_ref, meta_ref, mask_ref = refs[2 * outer : 2 * outer + 5]
    y_buf, out_ref, x_buf, w_buf, d_buf, hidden, acc, x_sem, w_sem, d_sem = refs[2 * outer + 5 :]
    local, cap2, half = xs[0][0].shape
    ff = gate_ref.shape[2]
    rows = mask_ref.shape[1]
    core = core_ref[0]

    depth = x_buf.shape[0]
    d_depth = d_buf.shape[0]
    span = 2 * half if outer * cap2 <= 512 else 512

    def x_copy(e, j, s):
        slot = (2 * e + j) % depth
        return pltpu.make_async_copy(
            xs[j][s].at[e], x_buf.at[slot, pl.ds(s * cap2, cap2), :], x_sem.at[slot, s]
        )

    def w_copy(e, j, i):
        slot = (2 * e + j) % depth
        at = pl.multiple_of((core ^ j) * half, half)
        return pltpu.make_async_copy(
            (gate_ref, up_ref)[i].at[e, pl.ds(at, half), :],
            w_buf.at[slot, :, pl.ds(i * ff, ff)],
            w_sem.at[slot, i],
        )

    def up_copies(e, j):
        return [x_copy(e, j, s) for s in range(outer)] + [w_copy(e, j, i) for i in range(2)]

    def d_copy(e):
        return pltpu.make_async_copy(down_ref.at[e], d_buf.at[e % d_depth], d_sem.at[e % d_depth])

    for e in range(depth // 2):
        for copy in up_copies(e, 0) + up_copies(e, 1):
            copy.start()
        if e < d_depth:
            d_copy(e).start()

    def one_expert(e, carry):
        acc[...] = jnp.zeros(acc.shape, F32)

        def one_half(j, inner):
            for side in range(2):

                @pl.when(j == side)
                def _():
                    for copy in up_copies(e, side):
                        copy.wait()

            slot = (2 * e + j) % depth
            acc[...] = acc[...] + jnp.dot(
                x_buf[slot], w_buf[slot], preferred_element_type=F32
            )
            for side in range(2):

                @pl.when((j == side) & (e + depth // 2 < local))
                def _():
                    for copy in up_copies(e + depth // 2, side):
                        copy.start()

            return inner

        lax.fori_loop(0, 2, one_half, 0)
        for s in range(outer):
            here = slice(s * cap2, (s + 1) * cap2)
            mask = one_hot_dynamic(meta_ref, 2 * s, e, rows)
            weight = jnp.concatenate(
                [meta_ref[2 * s + y, pl.ds(8 + e, 1), :] for y in range(2)], axis=1
            )
            weight = jnp.sum(jnp.where(mask, weight, 0.0), axis=1, keepdims=True)
            g = acc[here, 0:ff]
            u = acc[here, ff : 2 * ff]
            hidden[here, :] = (g / (1.0 + jnp.exp(-g)) * u * weight).astype(BF16)
        d_copy(e).wait()

        def columns(n, inner):
            cols = pl.ds(pl.multiple_of(n * span, span), span)
            y = jnp.dot(hidden[...], d_buf[e % d_depth, :, cols], preferred_element_type=F32).astype(BF16)
            for s in range(outer):
                y_buf[s, pl.ds(pl.multiple_of(e * cap2, cap2), cap2), cols] = y[
                    s * cap2 : (s + 1) * cap2
                ]
            return inner

        lax.fori_loop(0, 2 * half // span, columns, 0)

        @pl.when(e + d_depth < local)
        def _():
            d_copy(e + d_depth).start()

        return carry

    lax.fori_loop(0, local, one_expert, 0)

    combine_body([(1, 0)], core_ref, y_buf, mask_ref, out_ref)


def combine_body(parts, core_ref, y_ref, mask_ref, *out_refs):
    outer, all_rows, width = y_ref.shape
    for (flip, chunk), out_ref in zip(parts, out_refs):
        _, rows, part = out_ref.shape
        at = (core_ref[0] ^ flip) * (width // 2) + chunk * part
        cols = pl.ds(pl.multiple_of(at, part), part)
        for s in range(outer):
            both = mask_ref[2 * s : 2 * s + 2].reshape(2 * rows, all_rows)
            out = jnp.dot(both, y_ref[s, :, cols], preferred_element_type=F32).astype(BF16)
            out_ref[2 * s] = out[:rows]
            out_ref[2 * s + 1] = out[rows:]


def combine(core, y, mask, parts):
    count, rows, lanes = mask.shape
    part = y.shape[2] // 2 // CHUNKS
    vmem = pl.BlockSpec(memory_space=pltpu.VMEM)
    return pl.pallas_call(
        functools.partial(combine_body, parts),
        in_specs=[pl.BlockSpec(memory_space=pltpu.SMEM), vmem, vmem],
        out_specs=[vmem] * len(parts),
        out_shape=[jax.ShapeDtypeStruct((count, rows, part), BF16)] * len(parts),
        compiler_params=params(32),
        cost_estimate=cost(
            2 * count * rows * lanes * part * len(parts), 4 * count * rows * part * len(parts)
        ),
    )(core, y, mask)


def experts(core, own, sib, w_gate, w_up, w_down, meta, mask):
    outer = len(own)
    local, cap2, half = own[0].shape
    ff = w_gate.shape[2]
    count, rows, _ = mask.shape
    part = half // CHUNKS
    depth, d_depth = min(4, 2 * local), min(2, local)
    all_rows = outer * cap2
    vmem = pl.BlockSpec(memory_space=pltpu.VMEM)
    anywhere = pl.BlockSpec(memory_space=pl.ANY)
    return pl.pallas_call(
        functools.partial(experts_body, outer),
        in_specs=[pl.BlockSpec(memory_space=pltpu.SMEM)]
        + [anywhere] * (2 * outer + 3)
        + [vmem, vmem],
        out_specs=[vmem, vmem],
        out_shape=[
            pltpu.VMEM((outer, local * cap2, 2 * half), BF16),
            jax.ShapeDtypeStruct((count, rows, part), BF16),
        ],
        scratch_shapes=[
            pltpu.VMEM((depth, all_rows, half), BF16),
            pltpu.VMEM((depth, half, 2 * ff), BF16),
            pltpu.VMEM((d_depth, ff, 2 * half), BF16),
            pltpu.VMEM((all_rows, ff), BF16),
            pltpu.VMEM((all_rows, 2 * ff), F32),
            pltpu.SemaphoreType.DMA((depth, outer)),
            pltpu.SemaphoreType.DMA((depth, 2)),
            pltpu.SemaphoreType.DMA((d_depth,)),
        ],
        compiler_params=params(36 if all_rows <= 512 else 48),
        cost_estimate=cost(
            12 * local * all_rows * half * ff, 12 * local * half * ff + 8 * all_rows * half
        ),
    )(core, *own, *sib, w_gate, w_up, w_down, meta, mask)


def mask_body(local, meta_ref, out_ref):
    _, rows, lanes = out_ref.shape
    lane = lax.broadcasted_iota(jnp.int32, (rows, lanes), 1).astype(F32)
    y = pl.program_id(0) % 2
    hit = jnp.zeros((rows, lanes), F32)
    turned = jnp.concatenate([meta_ref[0]] * 8, axis=0).T
    for e in range(local):
        place = turned[:, e : e + 1]
        place = jnp.where(place >= 0, place + (e * 2 * CAP + y * CAP).astype(F32), -1.0)
        hit = jnp.where(lane == place, 1.0, hit)
    out_ref[0] = hit.astype(BF16)


def masks(meta, local):
    count, kinds, rows = meta.shape
    lanes = local * 2 * CAP
    return pl.pallas_call(
        functools.partial(mask_body, local),
        grid=(count,),
        in_specs=[pl.BlockSpec((1, kinds, rows), lambda i: (i, 0, 0))],
        out_specs=pl.BlockSpec((1, rows, lanes), lambda i: (i, 0, 0)),
        out_shape=jax.ShapeDtypeStruct((count, rows, lanes), BF16),
        compiler_params=params(8),
        cost_estimate=cost(1e6, count * rows * lanes * 4),
    )(meta)


def shards(ring, queries, keys, values, norm_gain, w_gate, w_up, w_down, expert_ids, gate_weights):
    local = w_gate.shape[0]
    outer = ring.outer
    me = lax.axis_index("ep")
    core = lax.axis_index("tp").astype(jnp.int32).reshape(1)
    blocks = jnp.asarray(ring.slots)[me]
    sort_scalars = jnp.concatenate([blocks, (me * local).astype(jnp.int32).reshape(1)])

    packed = ring.gather_small(pack(keys, values, expert_ids.T, gate_weights.T))
    k, v, meta = sort_slots(sort_scalars, [x for pair in packed for x in pair], local)
    mask = masks(meta, local)
    attention, squares = attend(blocks[:1], queries, k, v)
    normed = normalise(attention, squares, core_swap(squares), norm_gain.reshape(1, -1))
    slots = [ring.gather(normed[c], c == CHUNKS - 1) for c in range(CHUNKS)]
    own = [prepare(2 * s, [slots[c][s] for c in range(CHUNKS)], meta, local) for s in range(outer)]
    sib = [core_swap(x) for x in own]
    y, first = experts(core, own, sib, w_gate, w_up, w_down, meta, mask)
    away, here = [core_swap(first)], []
    for c in range(CHUNKS):
        if c + 1 < CHUNKS:
            mine, other = combine(core, y, mask, [(0, c), (1, c + 1)])
            here.append(mine)
            away.append(core_swap(other))
        else:
            here.append(combine(core, y, mask, [(0, c)])[0])

    def add(*terms):
        total = terms[0].astype(F32)
        for term in terms[1:]:
            total = total + term.astype(F32)
        return total.astype(BF16)

    firsts = [add(here[c][3], away[c][3]) for c in range(CHUNKS)]
    outs = []
    for c in range(CHUNKS):
        def both(slot):
            return [here[c][slot], away[c][slot]]

        by_ring = c == CHUNKS - 1
        order = list(range(1, outer)) + [0]
        moving, late = [], []
        if by_ring:
            late = [ring.ring(firsts[c])]
            other = []
        else:
            other = [ring.swap(firsts[c])]
        for at, s in enumerate(order):
            if s == 0:
                outs.append(add(normed[c], *both(0), *other, *moving))
                break
            after = order[at + 1]
            send = add(*both(2 * s), *other, *moving)
            extra = late if after == 2 else []
            swapped = add(*both(2 * after + 1), *extra)
            moving, other = [ring.ring(send)], [ring.swap(swapped)]
            pair = lax.optimization_barrier((moving[0], other[0]))
            moving, other = [pair[0]], [pair[1]]
    return jnp.concatenate(outs, axis=1)


def solution(mesh):
    ring = Ring(mesh.shape["ep"])
    return jax.shard_map(
        functools.partial(shards, ring),
        mesh=mesh,
        in_specs=(
            P(("groups", "ep"), "tp"),
            P(("groups", "ep"), "tp"),
            P(("groups", "ep"), "tp"),
            P("tp"),
            P("ep", None, "tp"),
            P("ep", None, "tp"),
            P("ep", "tp", None),
            P(("groups", "ep"), None),
            P(("groups", "ep"), None),
        ),
        out_specs=P(("groups", "ep"), "tp"),
        check_vma=False,
    )
```
